32 devices in a mesh: req: 8 (over y, x, core), head: 4 (over z).
Axes of the slice: x: 2, y: 2, z: 4, core: 2. Of those that a mesh axis runs over, the one named last changes fastest.
Arguments:
- tokens: bfloat16 [1024, 1536], P(('req', 'head')), may hold values from -6 to 6
- pre_gain: float32 [1536], replicated, may hold values from 0.1 to 1.9
- inner_weight: bfloat16 [1536, 2, 3072], P(None, None, 'head')
- shared_weight: bfloat16 [1536, 304], replicated, may hold values from -0.15625 to 0.15625
- conv_inner: float32 [4, 3072], P(None, 'head'), may hold values from -0.5 to 0.5
- conv_inner_bias: float32 [3072], P('head'), may hold values from -0.5 to 0.5
- conv_shared: float32 [4, 256], replicated, may hold values from -0.5 to 0.5
- conv_shared_bias: float32 [256], replicated, may hold values from -0.5 to 0.5
- step_bias: float32 [48], P('head'), may hold values from -4 to 0
- decay_log: float32 [48], P('head'), may hold values from 0 to 2.77
- skip_gain: float32 [48], P('head'), may hold values from 0.5 to 1.5
- gate_gain: float32 [3072], P('head'), may hold values from 0.1 to 1.9
- out_weight: bfloat16 [3072, 1536], P('head'), may hold values from -0.109375 to 0.109375
- states: bfloat16 [256, 48, 64, 128], P('req', 'head'), may hold values from -1.1953125 to 1.1953125
- edge_inner: bfloat16 [256, 3, 3072], P('req', None, 'head'), may hold values from -6 to 6
- edge_shared: bfloat16 [256, 3, 256], P('req'), may hold values from -6 to 6
- counts: int32 [256], P('req'), may hold values from 1 to 4, as said below
- mig_ids: int32 [8], replicated, may hold values from 0 to 255, as said below
- mig_dest: int32 [8], replicated, may hold values from 0 to 255, as said below
- reorder: int32 [256], replicated, may hold values from 0 to 255, as said below
Outputs:
- hidden_out: bfloat16 [1024, 1536], P(('req', 'head'))
- states_out: bfloat16 [256, 48, 64, 128], P('req', 'head')
- edge_inner_out: bfloat16 [256, 3, 3072], P('req', None, 'head')
- edge_shared_out: bfloat16 [256, 3, 256], P('req')
The draws below stay inside these ranges and needn't reach their ends.
Inputs may be any that keep to these rules, and one draw needn't show every extreme that they name: counts: each slot's token rows are r * 4 to r * 4 + 3 of tokens; the first counts[r] of them are real. mig_ids: distinct old slots listed by owner: entry i is one of the slots i * 32 to (i + 1) * 32 - 1, those held by index i of req. mig_dest: a reordering of the slots in mig_ids. reorder: a permutation of all slots. The 32 new slots j with j // 32 = d take at most 4 values reorder[j] of any one block of 32 slots, and exactly 4 of some block.
All inputs are finite; a program needn't handle non-finite values.
Results may differ from the reference program's by a relative error of at most 0.013.
Values may be sent and summed in bfloat16 or wider, within the bound.
No kernel may reach another device: no remote copies, remote signals or barrier semaphores. Data moves between devices by JAX's collectives and lax.ppermute only.
A program may use at most 128 MiB of HBM per device.

```python
import math
import jax
import jax.numpy as jnp
from jax import lax

D = 1536
HEADS = 48
HEAD_DIM = 64
STATE = 128
CONV = 4
TMAX = 4
REQ_DEV = 32
MIG_DEV = 1
INNER = 3072
REQUESTS = 256


def draw_inner_weight(key, part):
    columns = jnp.arange(HEADS * HEAD_DIM, dtype=jnp.float32) / (HEADS * HEAD_DIM)
    values = jax.random.normal(key, (D, 2, HEADS * HEAD_DIM), jnp.float32)
    factor = jnp.exp(math.log(3.0) * (columns - 0.5))
    return (values * factor * (1.0 / math.sqrt(D))).astype(jnp.bfloat16)


def migration_lists(key):
    folded = jax.random.fold_in(key, 17)
    first_key, second_key = jax.random.split(folded)
    groups = REQUESTS // REQ_DEV

    def choose_local(member):
        return jax.random.permutation(member, REQ_DEV)[:MIG_DEV]
    chosen = jax.vmap(choose_local)(jax.random.split(first_key, groups))
    listed = (jnp.arange(groups, dtype=jnp.int32)[:, None] * REQ_DEV + chosen.astype(jnp.int32)).reshape(-1)
    shuffled = listed[jax.random.permutation(second_key, groups * MIG_DEV)]
    return (listed.astype(jnp.int32), shuffled.astype(jnp.int32))


def draw_mig_ids(key, part):
    return migration_lists(key)[0]


def draw_mig_dest(key, part):
    return migration_lists(key)[1]


def draw_reorder(key, part):
    groups = REQUESTS // REQ_DEV
    first_key, second_key = jax.random.split(jax.random.fold_in(key, 3))

    def local_order(member):
        return jax.random.permutation(member, REQ_DEV).astype(jnp.int32)
    picked = jax.vmap(local_order)(jax.random.split(first_key, groups))
    placed = jax.vmap(local_order)(jax.random.split(second_key, groups))
    owners = jnp.arange(groups, dtype=jnp.int32)[:, None]
    if REQ_DEV < groups:
        spacing = groups // REQ_DEV
        offsets = jnp.where(picked == 0, groups - 1, picked * spacing).astype(jnp.int32)
    else:
        offsets = (picked % groups).astype(jnp.int32)
    source_owner = (owners + offsets) % groups
    source_local = placed[source_owner, picked]
    return (source_owner * REQ_DEV + source_local).reshape(-1).astype(jnp.int32)


def draw_counts(key, part):
    first_key, second_key, third_key = jax.random.split(jax.random.fold_in(key, 5), 3)
    levels = jax.random.randint(first_key, (REQUESTS,), 0, 16)
    result = 1 + (levels >= 8).astype(jnp.int32) + (levels >= 12).astype(jnp.int32) + (levels >= 14).astype(jnp.int32)
    longest_at = jax.random.randint(second_key, (), 0, REQUESTS)
    shortest_at = (longest_at + 1 + jax.random.randint(third_key, (), 0, REQUESTS - 1)) % REQUESTS
    result = result.at[longest_at].set(TMAX).at[shortest_at].set(1)
    return result.astype(jnp.int32)


def shard_levels(key, shape, cuts, low, largest):
    gain = 1.0
    for axis_at, blocks in cuts:
        draws = jax.random.uniform(jax.random.fold_in(jax.random.fold_in(key, 6), axis_at), (blocks,), jnp.float32, low / len(cuts), largest / len(cuts))
        gain = gain * jnp.repeat(jnp.exp(draws), shape[axis_at] // blocks).reshape((-1,) + (1,) * (len(shape) - 1 - axis_at))
    return gain


def scatter_about(stream_key, shape, scale, most, cuts=(), held_as=jnp.bfloat16):
    values = jax.random.normal(stream_key, shape, jnp.float32) * scale
    if len(cuts) > 0:
        values = shard_levels(stream_key, shape, cuts, -0.22, 0.18) * values
    return jnp.clip(values, min=-most, max=most).astype(held_as)


def setup_inputs(seed: int = 0) -> dict:
    keys = jax.random.split(jax.random.key(seed), 21)
    return {
        "tokens": scatter_about(keys[0], (REQUESTS * TMAX, D), 1.0, 6.0, ((0, 32),)),
        "pre_gain": jnp.clip(1.0 + 0.18 * jax.random.normal(keys[1], (D,), jnp.float32), 0.1, 1.9),
        "inner_weight": draw_inner_weight(jax.random.fold_in(keys[20], 71), 0),
        "shared_weight": scatter_about(keys[3], (D, 2 * STATE + HEADS), D ** -0.5, 0.15625),
        "conv_inner": jnp.clip(jax.random.uniform(keys[4], (CONV, INNER), jnp.float32, -0.5, 0.5) * shard_levels(keys[4], (CONV, INNER), ((1, 4),), -0.4, 0.0), -0.5, 0.5),
        "conv_inner_bias": jnp.clip(jax.random.uniform(keys[5], (INNER,), jnp.float32, -0.5, 0.5) * shard_levels(keys[5], (INNER,), ((0, 4),), -0.4, 0.0), -0.5, 0.5),
        "conv_shared": jnp.clip(jax.random.uniform(keys[6], (CONV, 2 * STATE), jnp.float32, -0.5, 0.5), -0.5, 0.5),
        "conv_shared_bias": jnp.clip(jax.random.uniform(keys[7], (2 * STATE,), jnp.float32, -0.5, 0.5), -0.5, 0.5),
        "step_bias": jnp.clip(-4.0 + 4.0 * jax.random.uniform(keys[8], (HEADS,), jnp.float32) ** shard_levels(keys[8], (HEADS,), ((0, 4),), -0.2, 0.2), -4.0, 0.0),
        "decay_log": jnp.clip(2.77 * jax.random.uniform(keys[9], (HEADS,), jnp.float32) ** shard_levels(keys[9], (HEADS,), ((0, 4),), -0.2, 0.2), 0.0, 2.77),
        "skip_gain": jnp.clip(0.5 + 1.0 * jax.random.uniform(keys[10], (HEADS,), jnp.float32) ** shard_levels(keys[10], (HEADS,), ((0, 4),), -0.2, 0.2), 0.5, 1.5),
        "gate_gain": jnp.clip(1.0 + 0.18 * jax.random.normal(keys[11], (INNER,), jnp.float32), 0.1, 1.9),
        "out_weight": scatter_about(keys[12], (INNER, D), INNER ** -0.5, 0.109375, ((0, 4),)),
        "states": scatter_about(keys[13], (REQUESTS, HEADS, HEAD_DIM, STATE), 0.2, 1.1953125, ((0, 8), (1, 4))),
        "edge_inner": scatter_about(keys[14], (REQUESTS, CONV - 1, INNER), 1.0, 6.0, ((0, 8), (2, 4))),
        "edge_shared": scatter_about(keys[15], (REQUESTS, CONV - 1, 2 * STATE), 1.0, 6.0, ((0, 8),)),
        "counts": draw_counts(jax.random.fold_in(keys[20], 71), 0),
        "mig_ids": draw_mig_ids(jax.random.fold_in(keys[20], 71), 0),
        "mig_dest": draw_mig_dest(jax.random.fold_in(keys[20], 71), 0),
        "reorder": draw_reorder(jax.random.fold_in(keys[20], 71), 0),
    }


EPS = 1e-05

def advance(carried, step_now, inputs_now, entry_now, readout_now, decay, skip_gain):
    factor = jnp.exp(step_now * decay)
    carried = carried * factor[:, :, None, None] + (step_now[:, :, None] * inputs_now)[:, :, :, None] * entry_now[:, None, None, :]
    produced = jnp.einsum('khpn,kn->khp', carried, readout_now, precision=lax.Precision.HIGHEST)
    return (carried, produced + skip_gain[None, :, None] * inputs_now)

def depthwise(edge, fresh, weight, offset_bias):
    sequence = jnp.concatenate([edge, fresh], axis=1).astype(jnp.float32)
    window = fresh.shape[1]
    summed = sequence[:, 0:window] * weight[0]
    for offset in range(1, weight.shape[0]):
        summed = summed + sequence[:, offset:offset + window] * weight[offset]
    return jax.nn.silu(summed + offset_bias)

def new_edge(edge, fresh, counts):
    sequence = jnp.concatenate([edge, fresh], axis=1)
    keep_rows = edge.shape[1]
    result = edge
    for length in range(1, fresh.shape[1] + 1):
        result = jnp.where((counts == length)[:, None, None], sequence[:, length:length + keep_rows], result)
    return result

def reference(tokens, pre_gain, inner_weight, shared_weight, conv_inner, conv_inner_bias, conv_shared, conv_shared_bias, step_bias, decay_log, skip_gain, gate_gain, out_weight, states, edge_inner, edge_shared, counts, mig_ids, mig_dest, reorder):
    all_slots = jnp.arange(REQUESTS, dtype=jnp.int32)
    source = all_slots.at[mig_dest].set(mig_ids)
    anchor = source[reorder]
    moved_states = states[anchor]
    moved_inner = edge_inner[anchor]
    moved_shared = edge_shared[anchor]
    rows_in = tokens.astype(jnp.float32)
    normed = (rows_in * lax.rsqrt(lax.optimization_barrier(jnp.mean(rows_in * rows_in, axis=-1, keepdims=True)) + EPS) * pre_gain).astype(jnp.bfloat16)
    gate_part = jnp.dot(normed, inner_weight[:, 0, :], preferred_element_type=jnp.float32).astype(jnp.bfloat16)
    value_part = jnp.dot(normed, inner_weight[:, 1, :], preferred_element_type=jnp.float32).astype(jnp.bfloat16)
    shared_part = jnp.dot(normed, shared_weight, preferred_element_type=jnp.float32).astype(jnp.bfloat16)
    gate_part = gate_part.reshape(REQUESTS, TMAX, INNER)
    value_part = value_part.reshape(REQUESTS, TMAX, INNER)
    shared_part = shared_part.reshape(REQUESTS, TMAX, 2 * STATE + HEADS)
    fresh_shared = shared_part[:, :, :2 * STATE]
    edge_inner_out = new_edge(moved_inner, value_part, counts)
    edge_shared_out = new_edge(moved_shared, fresh_shared, counts)
    mixed_inner = depthwise(moved_inner, value_part, conv_inner, conv_inner_bias)
    mixed_shared = depthwise(moved_shared, fresh_shared, conv_shared, conv_shared_bias)
    valid = jnp.arange(TMAX)[None, :] < counts[:, None]
    step_size = jax.nn.softplus(shared_part[:, :, 2 * STATE:].astype(jnp.float32) + step_bias)
    step_size = jnp.where(valid[:, :, None], step_size, 0.0)
    decay = -jnp.exp(decay_log)
    inputs = mixed_inner.reshape(REQUESTS, TMAX, HEADS, HEAD_DIM)

    def run_block(block):
        carried, step_block, input_block, shared_block = block
        carried = carried.astype(jnp.float32)
        collected = []
        for position in range(TMAX):
            carried, produced = advance(carried, step_block[:, position], input_block[:, position], shared_block[:, position, :STATE], shared_block[:, position, STATE:], decay, skip_gain)
            collected.append(produced)
        return (carried.astype(jnp.bfloat16), jnp.stack(collected, axis=1))
    block_count = REQUESTS // REQ_DEV

    def split_blocks(array):
        return array.reshape((block_count, REQ_DEV) + array.shape[1:])
    final_states, outputs = lax.map(run_block, (split_blocks(moved_states), split_blocks(step_size), split_blocks(inputs), split_blocks(mixed_shared)))
    final_states = final_states.reshape(states.shape)
    outputs = outputs.reshape(REQUESTS, TMAX, INNER)
    gated = outputs * jax.nn.silu(gate_part.astype(jnp.float32))
    square_sum = lax.optimization_barrier(jnp.sum(gated * gated, axis=-1, keepdims=True))
    scaled = gated * lax.rsqrt(square_sum / INNER + EPS) * gate_gain
    scaled = jnp.where(valid[:, :, None], scaled, 0.0).astype(jnp.bfloat16).reshape(REQUESTS * TMAX, INNER)
    mixer = jnp.dot(scaled, out_weight, preferred_element_type=jnp.float32)
    hidden_out = (rows_in + mixer).astype(jnp.bfloat16)
    return (hidden_out, final_states, edge_inner_out, edge_shared_out)
```

```python
import functools

import jax
import jax.numpy as jnp
from jax import lax
from jax.experimental import pallas as pl
from jax.experimental.pallas import tpu as pltpu
from jax.sharding import PartitionSpec as P

EPS = 1e-05
F32 = jnp.float32
BF16 = jnp.bfloat16
VMEM_BYTES = 16 * 1024 * 1024
HBM = pl.BlockSpec(memory_space=pl.ANY)
SMEM = pl.BlockSpec(memory_space=pltpu.SMEM)
VMEM = pl.BlockSpec(memory_space=pltpu.VMEM)


def peer_of(index, step, size):
    if size & (size - 1) == 0:
        return index ^ step
    return lax.rem(index + step, size)


def origin_of(index, step, size):
    if size & (size - 1) == 0:
        return index ^ step
    return lax.rem(index - step + size, size)


def permute(value, axis, step):
    size = lax.axis_size(axis)
    pairs = [(i, i ^ step if size & (size - 1) == 0 else (i + step) % size) for i in range(size)]
    return lax.ppermute(value, axis, pairs)


def fill_sources(count, ids_ref, dest_ref, source):
    def fill(slot, carry):
        source[slot] = slot
        return carry

    lax.fori_loop(0, count, fill, 0)

    def migrate(entry, carry):
        source[dest_ref[entry]] = ids_ref[entry]
        return carry

    lax.fori_loop(0, ids_ref.shape[0], migrate, 0)


def pack_kernel(
    groups,
    slots,
    capacity,
    edge_block,
    chunk,
    device_ref,
    ids_ref,
    dest_ref,
    reorder_ref,
    inner_ref,
    shared_ref,
    states_ref,
    out_edges,
    recv_rows,
    out_states,
    source,
    target,
    seen,
    staged,
    read_done,
    write_done,
):
    first = device_ref[0] * slots
    reads = [
        pltpu.make_async_copy(
            states_ref.at[pl.ds(part * chunk, chunk)], staged.at[pl.ds(part * chunk, chunk)], read_done.at[part]
        )
        for part in range(slots // chunk)
    ]
    for read in reads:
        read.start()
    fill_sources(groups * slots, ids_ref, dest_ref, source)

    def to_peer(peer, carry):
        def one(slot, rank):
            local = source[reorder_ref[peer * slots + slot]] - first
            mine = jnp.logical_and(local >= 0, local < slots)

            @pl.when(mine)
            def _():
                target[local] = peer * edge_block + rank

            return rank + mine.astype(jnp.int32)

        lax.fori_loop(0, slots, one, 0, unroll=4)
        return carry

    lax.fori_loop(0, groups, to_peer, 0)

    def clear(group, carry):
        seen[group] = 0
        return carry

    lax.fori_loop(0, groups, clear, 0)

    def receive(slot, carry):
        owner = lax.div(source[reorder_ref[first + slot]], slots)
        rank = seen[owner]
        recv_rows[slot] = owner * edge_block + rank
        seen[owner] = rank + 1
        return carry

    lax.fori_loop(0, slots, receive, 0)

    for part in range(slots // chunk):
        reads[part].wait()
        for slot in range(part * chunk, (part + 1) * chunk):
            place = target[slot]
            row = lax.div(place, edge_block) * capacity + lax.rem(place, edge_block)
            pltpu.make_async_copy(staged.at[slot], out_states.at[row], write_done.at[0]).start()

    keep = inner_ref.shape[0]
    rows = groups * edge_block
    lane = lax.broadcasted_iota(jnp.int32, (1, slots), 1)
    places = jnp.zeros((1, slots), jnp.int32)
    for slot in range(slots):
        places = jnp.where(lane == slot, target[slot], places)
    row = lax.broadcasted_iota(jnp.int32, (rows, slots), 0)
    width = inner_ref.shape[2]
    inner_sum = jnp.zeros((rows, width), F32)
    shared_sum = jnp.zeros((rows, shared_ref.shape[2]), F32)
    for k in range(keep):
        pick = jnp.where(row == places + k * capacity, 1.0, 0.0).astype(BF16)
        inner_sum = inner_sum + jnp.dot(pick, inner_ref[k], preferred_element_type=F32)
        shared_sum = shared_sum + jnp.dot(pick, shared_ref[k], preferred_element_type=F32)
    out_edges[:, :width] = inner_sum.astype(BF16)
    out_edges[:, width:] = shared_sum.astype(BF16)
    pltpu.make_async_copy(staged, out_states.at[pl.ds(0, slots)], write_done.at[0]).wait()


def pack(device, mig_ids, mig_dest, reorder, states, edge_inner, edge_shared, groups, capacity, edge_block):
    slots = states.shape[0]
    width = edge_inner.shape[2] + edge_shared.shape[2]
    chunk = 4
    return pl.pallas_call(
        functools.partial(pack_kernel, groups, slots, capacity, edge_block, chunk),
        out_shape=(
            jax.ShapeDtypeStruct((groups * edge_block, width), BF16),
            jax.ShapeDtypeStruct((slots,), jnp.int32),
            jax.ShapeDtypeStruct((groups * capacity,) + states.shape[1:], states.dtype),
        ),
        in_specs=[SMEM] * 4 + [VMEM] * 2 + [HBM],
        out_specs=(VMEM, SMEM, HBM),
        scratch_shapes=[
            pltpu.SMEM((groups * slots,), jnp.int32),
            pltpu.SMEM((slots,), jnp.int32),
            pltpu.SMEM((groups,), jnp.int32),
            pltpu.VMEM(states.shape, states.dtype),
            pltpu.SemaphoreType.DMA((slots // chunk,)),
            pltpu.SemaphoreType.DMA((1,)),
        ],
        compiler_params=pltpu.CompilerParams(vmem_limit_bytes=VMEM_BYTES),
        name="pack",
    )(device, mig_ids, mig_dest, reorder, edge_inner.transpose(1, 0, 2), edge_shared.transpose(1, 0, 2), states)


def shift_rows(value, by):
    by = by % value.shape[0]
    return pltpu.roll(value, by, 0) if by else value


def mix(edge, fresh, weight, bias, token):
    taps = weight.shape[0]
    summed = fresh * weight[taps - 1 : taps] + bias
    for tap in range(taps - 1):
        back = taps - 1 - tap
        moved = jnp.where(token >= back, shift_rows(fresh, back), shift_rows(edge, -tap))
        summed = summed + moved * weight[tap : tap + 1]
    return summed / (1.0 + jnp.exp(-summed))


def latest(edge, fresh, counts, token, window):
    keep = window - 1
    result = edge
    for length in range(1, window + 1):
        chosen = jnp.where(token + length < keep, shift_rows(edge, -length), shift_rows(fresh, keep - length))
        result = jnp.where(counts == length, chosen, result)
    return result


def token_kernel(
    window,
    heads,
    head_dim,
    state_dim,
    capacity,
    device_ref,
    skip_ref,
    recv_ref,
    rows_ref,
    shared_ref,
    edges_ref,
    counts_ref,
    conv_inner_ref,
    inner_bias_ref,
    conv_shared_ref,
    shared_bias_ref,
    step_bias_ref,
    decay_log_ref,
    moved_ref,
    entry_ref,
    readout_ref,
    within_ref,
    decay_ref,
    gate_ref,
    new_inner_ref,
    new_shared_ref,
):
    inner = heads * head_dim
    rows = rows_ref.shape[0]
    wide = lax.broadcasted_iota(jnp.int32, (rows, 1), 0)
    token = lax.rem(wide, window)
    counts = counts_ref[...]
    valid = token < counts

    arrived = edges_ref.shape[0]
    place = jnp.zeros((rows, 1), jnp.int32)
    for slot in range(rows // window):
        place = jnp.where(lax.div(wide, window) == slot, recv_ref[slot], place)
    pick = lax.broadcasted_iota(jnp.int32, (rows, arrived), 1) == place + token * capacity
    pick = jnp.logical_and(pick, token < window - 1)
    edges = jnp.dot(jnp.where(pick, 1.0, 0.0).astype(BF16), edges_ref[...], preferred_element_type=F32)

    gate = rows_ref[:, :inner].astype(F32)
    gate_ref[...] = jnp.where(valid, gate / (1.0 + jnp.exp(-gate)), 0.0)

    value = rows_ref[:, inner:].astype(F32)
    edge = edges[:, :inner]
    new_inner_ref[...] = latest(edge, value, counts, token, window).astype(BF16)
    mixed = mix(edge, value, conv_inner_ref[...], inner_bias_ref[...], token)

    fresh = shared_ref[:, : 2 * state_dim].astype(F32)
    edge = edges[:, inner:]
    new_shared_ref[...] = latest(edge, fresh, counts, token, window).astype(BF16)
    shared = mix(edge, fresh, conv_shared_ref[...], shared_bias_ref[...], token)
    entry = shared[:, :state_dim]
    readout = shared[:, state_dim:]
    entry_ref[...] = entry.astype(BF16)
    readout_t = readout.T.astype(BF16)
    readout_ref[...] = readout_t

    raw = shared_ref[:, 2 * state_dim :]
    all_heads = raw.shape[1]
    from_head = lax.broadcasted_iota(jnp.int32, (all_heads, rows), 0)
    to_lane = lax.broadcasted_iota(jnp.int32, (all_heads, rows), 1)
    pick = jnp.logical_and(from_head == to_lane + device_ref[1] * heads, to_lane < heads)
    raw = jnp.dot(raw, pick.astype(BF16), preferred_element_type=F32) + step_bias_ref[...]
    step = jnp.maximum(raw, 0.0) + jnp.log(1.0 + jnp.exp(-jnp.abs(raw)))
    step = jnp.where(valid, step, 0.0)
    drop = step * -jnp.exp(decay_log_ref[...])
    total = drop
    after = drop
    reach = 1
    while reach < window:
        total = total + jnp.where(token >= reach, shift_rows(total, reach), 0.0)
        after = after + jnp.where(token + reach < window, shift_rows(after, -reach), 0.0)
        reach *= 2
    after = jnp.where(token + 1 < window, shift_rows(after, -1), 0.0)
    total_t = total.T
    decay_ref[...] = jnp.exp(total_t)[: decay_ref.shape[0]]
    carry_t = (step * jnp.exp(after)).T

    slot_a = lax.div(lax.broadcasted_iota(jnp.int32, (rows, rows), 0), window)
    slot_b = lax.div(lax.broadcasted_iota(jnp.int32, (rows, rows), 1), window)
    row_a = lax.broadcasted_iota(jnp.int32, (rows, rows), 0)
    row_b = lax.broadcasted_iota(jnp.int32, (rows, rows), 1)
    causal = jnp.logical_and(slot_a == slot_b, row_a <= row_b)
    overlap = jnp.dot(entry.astype(BF16), readout_t, preferred_element_type=F32)
    overlap = jnp.where(causal, overlap, 0.0)
    for block in range(inner // rows):
        turned = mixed[:, block * rows : (block + 1) * rows].T
        for part in range(rows // head_dim):
            head = block * (rows // head_dim) + part
            mine = turned[part * head_dim : (part + 1) * head_dim]
            here = pl.ds(head * head_dim, head_dim)
            moved_ref[here, :] = (mine * carry_t[head : head + 1]).astype(BF16)
            gap = jnp.minimum(total_t[head : head + 1] - total[:, head : head + 1], 0.0)
            weight = overlap * jnp.exp(gap) * step[:, head : head + 1]
            within_ref[here, :] = skip_ref[head] * mine + jnp.dot(
                mine.astype(BF16), weight.astype(BF16), preferred_element_type=F32
            )


def token_part(
    device, skip_gain, recv_rows, rows, shared, edges, counts, conv_inner, inner_bias, conv_shared, shared_bias, step_bias, decay_log, window, heads, head_dim, state_dim, capacity
):
    count = rows.shape[0]
    inner = heads * head_dim
    padded = -(-heads // 8) * 8
    shape = jax.ShapeDtypeStruct
    return pl.pallas_call(
        functools.partial(token_kernel, window, heads, head_dim, state_dim, capacity),
        out_shape=(
            shape((inner, count), BF16),
            shape((count, state_dim), BF16),
            shape((state_dim, count), BF16),
            shape((inner, count), F32),
            shape((padded, count), F32),
            shape((count, inner), F32),
            shape((count, inner), BF16),
            shape((count, 2 * state_dim), BF16),
        ),
        in_specs=[SMEM] * 3 + [VMEM] * 10,
        out_specs=(VMEM,) * 8,
        compiler_params=pltpu.CompilerParams(vmem_limit_bytes=VMEM_BYTES),
        name="token_rows",
    )(device, skip_gain, recv_rows, rows, shared, edges, counts, conv_inner, inner_bias, conv_shared, shared_bias, step_bias, decay_log)


def state_kernel(window, batch, rows_ref, decay_smem, *refs):
    del rows_ref
    pages = refs[:batch]
    moved_ref, entry_ref, readout_ref, within_ref, decay_ref, gate_ref, gain_ref, weight_ref, out_ref, message_ref, read_sum = refs[batch:]
    step = pl.program_id(0)
    heads, head_dim, state_dim = pages[0].shape[1:]
    inner = heads * head_dim
    count = entry_ref.shape[0]
    entry = entry_ref[...]
    readout = readout_ref[...]
    row_slot = lax.div(lax.broadcasted_iota(jnp.int32, (count, state_dim), 0), window)
    lane_slot = lax.div(lax.broadcasted_iota(jnp.int32, (state_dim, count), 1), window)
    first = step * batch
    zero = jnp.zeros((), BF16)
    entries = jnp.concatenate([jnp.where(row_slot == first + q, entry, zero) for q in range(batch)], axis=1)
    readouts = jnp.concatenate([jnp.where(lane_slot == first + q, readout, zero) for q in range(batch)], axis=0)
    held = jnp.concatenate([page[0].reshape(inner, state_dim) for page in pages], axis=1)
    read = jnp.dot(held, readouts, preferred_element_type=F32)

    @pl.when(step == 0)
    def _():
        read_sum[...] = read

    @pl.when(step > 0)
    def _():
        read_sum[...] += read

    added = jnp.dot(moved_ref[...], entries, preferred_element_type=F32)
    for q in range(batch):
        lane = (first + q) * window + window - 1
        for head in range(heads):
            here = slice(head * head_dim, (head + 1) * head_dim)
            kept = pages[q][0, head].astype(F32) * decay_smem[head, lane]
            out_ref[q, head] = (kept + added[here, q * state_dim : (q + 1) * state_dim]).astype(BF16)

    @pl.when(step == pl.num_programs(0) - 1)
    def _():
        decay = decay_ref[...]
        blocks = []
        for block in range(inner // count):
            parts = []
            for part in range(count // head_dim):
                head = block * (count // head_dim) + part
                here = pl.ds(head * head_dim, head_dim)
                parts.append(read_sum[here, :] * decay[head : head + 1] + within_ref[here, :])
            blocks.append(jnp.concatenate(parts, axis=0).T)
        gated = jnp.concatenate(blocks, axis=1) * gate_ref[...]
        squares = jnp.sum(gated * gated, axis=1, keepdims=True)
        high = squares.astype(BF16)
        low = (squares - high.astype(F32)).astype(BF16)
        scaled = (gated * gain_ref[...]).astype(BF16)
        width = weight_ref.shape[1]
        message_ref[:, :width] = jnp.dot(scaled, weight_ref[...], preferred_element_type=F32).astype(BF16)
        lane = lax.broadcasted_iota(jnp.int32, (count, message_ref.shape[1] - width), 1)
        message_ref[:, width:] = jnp.where(lane == 0, high, jnp.where(lane == 1, low, zero))


def state_part(recv_rows, decay, received, moved, entry, readout, within, gate, gain, out_weight, window):
    slots = recv_rows.shape[0]
    page = received.shape[1:]
    batch = 4
    steps = slots // batch
    count, inner = gate.shape
    width = out_weight.shape[1]

    def page_spec(q):
        return pl.BlockSpec((1,) + page, lambda i, rows, q=q: (rows[i * batch + q], 0, 0, 0))

    def whole(array):
        return pl.BlockSpec(array.shape, lambda i, rows: (0,) * array.ndim)

    return pl.pallas_call(
        functools.partial(state_kernel, window, batch),
        grid_spec=pltpu.PrefetchScalarGridSpec(
            num_scalar_prefetch=1,
            grid=(steps,),
            in_specs=[pl.BlockSpec(memory_space=pltpu.SMEM)]
            + [page_spec(q) for q in range(batch)]
            + [whole(a) for a in (moved, entry, readout, within, decay, gate, gain, out_weight)],
            out_specs=(
                pl.BlockSpec((batch,) + page, lambda i, rows: (i, 0, 0, 0)),
                pl.BlockSpec((count, width + 128), lambda i, rows: (0, 0)),
            ),
            scratch_shapes=[pltpu.VMEM((inner, count), F32)],
        ),
        out_shape=(
            jax.ShapeDtypeStruct((slots,) + page, BF16),
            jax.ShapeDtypeStruct((count, width + 128), BF16),
        ),
        compiler_params=pltpu.CompilerParams(vmem_limit_bytes=VMEM_BYTES),
        name="states",
    )(recv_rows, decay, *([received] * batch), moved, entry, readout, within, decay, gate, gain, out_weight)


def local(
    tokens,
    pre_gain,
    inner_weight,
    shared_weight,
    conv_inner,
    conv_inner_bias,
    conv_shared,
    conv_shared_bias,
    step_bias,
    decay_log,
    skip_gain,
    gate_gain,
    out_weight,
    states,
    edge_inner,
    edge_shared,
    counts,
    mig_ids,
    mig_dest,
    reorder,
):
    slots, heads, head_dim, state_dim = states.shape
    inner = heads * head_dim
    groups = lax.axis_size("req")
    shares = lax.axis_size("head")
    request_index = lax.axis_index("req")
    head_index = lax.axis_index("head")
    device = jnp.stack([request_index, head_index]).astype(jnp.int32)
    own_rows = tokens.shape[0]
    window = own_rows * shares // slots
    width = tokens.shape[1]
    capacity = -(-slots // groups) + mig_ids.shape[0] // groups

    keep = edge_inner.shape[1]
    edge_block = -(-keep * capacity // 16) * 16
    send_edges, recv_rows, send_states = pack(
        device, mig_ids, mig_dest, reorder, states, edge_inner, edge_shared, groups, capacity, edge_block
    )
    exchange = functools.partial(lax.all_to_all, axis_name="req", split_axis=0, concat_axis=0, tiled=True)
    edges = exchange(send_edges)
    send_states, edges = lax.optimization_barrier((send_states, edges))
    received = exchange(send_states)

    rows_in = tokens.astype(F32)
    normed = (rows_in * lax.rsqrt(jnp.mean(rows_in * rows_in, axis=-1, keepdims=True) + EPS) * pre_gain).astype(BF16)
    all_rows = jnp.zeros((own_rows * shares, width), BF16)
    for step in range(shares):
        piece = permute(normed, "head", step) if step else normed
        start = origin_of(head_index, step, shares) * own_rows
        all_rows = lax.dynamic_update_slice_in_dim(all_rows, piece, start, 0)
    inner_flat = inner_weight.reshape(width, 2 * inner)
    inner_rows = jnp.dot(all_rows, inner_flat, preferred_element_type=F32).astype(BF16)
    shared_rows = jnp.dot(all_rows, shared_weight, preferred_element_type=F32).astype(BF16)

    lanes = slots * window

    def in_lanes(vector):
        return jnp.pad(vector, (0, lanes - heads)).reshape(1, lanes)

    moved, entry, readout, within, decay, gate, new_inner, new_shared = token_part(
        device,
        skip_gain,
        recv_rows,
        inner_rows,
        shared_rows,
        edges,
        jnp.repeat(counts, window).reshape(lanes, 1),
        conv_inner,
        conv_inner_bias.reshape(1, -1),
        conv_shared,
        conv_shared_bias.reshape(1, -1),
        in_lanes(step_bias),
        in_lanes(decay_log),
        window,
        heads,
        head_dim,
        state_dim,
        capacity,
    )
    page_rows = lax.div(recv_rows, edge_block) * capacity + lax.rem(recv_rows, edge_block)
    edge_inner_out = new_inner.reshape(slots, window, inner)[:, :keep]
    edge_shared_out = new_shared.reshape(slots, window, 2 * state_dim)[:, :keep]

    states_out, message = state_part(
        page_rows, decay, received, moved, entry, readout, within, gate, gate_gain.reshape(1, -1), out_weight, window
    )
    total = jnp.zeros((own_rows, message.shape[1]), F32)
    for step in range(shares):
        start = peer_of(head_index, step, shares) * own_rows
        piece = lax.dynamic_slice_in_dim(message, start, own_rows)
        if step:
            piece = permute(piece, "head", step)
        total = total + piece.astype(F32)
    squares = total[:, width : width + 1] + total[:, width + 1 : width + 2]
    mixer = total[:, :width] * lax.rsqrt(squares / (inner * shares) + EPS)
    hidden_out = (rows_in + mixer).astype(BF16)
    return (hidden_out, states_out, edge_inner_out, edge_shared_out)


def solution(mesh):
    placed = (
        P(("req", "head"), None),
        P(),
        P(None, None, "head"),
        P(),
        P(None, "head"),
        P("head"),
        P(),
        P(),
        P("head"),
        P("head"),
        P("head"),
        P("head"),
        P("head", None),
        P("req", "head", None, None),
        P("req", None, "head"),
        P("req", None, None),
        P("req"),
        P(),
        P(),
        P(),
    )
    return jax.shard_map(
        local,
        mesh=mesh,
        in_specs=placed,
        out_specs=(
            P(("req", "head"), None),
            P("req", "head", None, None),
            P("req", None, "head"),
            P("req", None, None),
        ),
        check_vma=False,
    )
```

```python
import functools

import jax
import jax.numpy as jnp
from jax import lax
from jax.experimental import pallas as pl
from jax.experimental.pallas import tpu as pltpu
from jax.sharding import PartitionSpec as P

EPS = 1e-05
F32 = jnp.float32
BF16 = jnp.bfloat16
VMEM_BYTES = 63 * 1024 * 1024
CHEAP = pl.CostEstimate(flops=1, bytes_accessed=1, transcendentals=0)
HBM = pl.BlockSpec(memory_space=pltpu.HBM)
SMEM = pl.BlockSpec(memory_space=pltpu.SMEM)
VMEM = pl.BlockSpec(memory_space=pltpu.VMEM)


def peer_of(index, step, size):
    if size & (size - 1) == 0:
        return index ^ step
    return lax.rem(index + step, size)


def origin_of(index, step, size):
    if size & (size - 1) == 0:
        return index ^ step
    return lax.rem(index - step + size, size)


def permute(value, axis, step):
    size = lax.axis_size(axis)
    pairs = [(i, i ^ step if size & (size - 1) == 0 else (i + step) % size) for i in range(size)]
    return lax.ppermute(value, axis, pairs)


def invert(order, place):
    def one(slot, carry):
        place[order[slot]] = slot
        return carry

    lax.fori_loop(0, order.shape[0], one, 0, unroll=16)


def fetch(pairs, done, first=0):
    copies = [pltpu.make_async_copy(source, target, done.at[first + n]) for n, (source, target) in enumerate(pairs)]
    for copy in copies:
        copy.start()
    return copies


def pack_kernel(
    groups,
    slots,
    early,
    capacity,
    edge_block,
    chunk,
    ids_hbm,
    dest_hbm,
    reorder_hbm,
    inner_hbm,
    shared_hbm,
    states_ref,
    slot_of,
    recv_rows,
    new_slots,
    out_edges,
    leaving,
    out_late,
    *refs,
):
    out_early = refs[: groups - 1] if early else []
    ids, dest, reorder, place, edge_place, seen, kept, staged, inner, shared, read_done, write_done, small_done = refs[len(out_early) :]
    stride = slots // groups
    device = lax.axis_index("req")
    first = device * slots
    small = fetch(((ids_hbm, ids), (dest_hbm, dest), (reorder_hbm, reorder)), small_done)
    parts = [pl.ds(part * chunk, chunk) for part in range(slots // chunk)]
    reads = fetch([(states_ref.at[part], staged.at[part]) for part in parts], read_done)
    edges = fetch(((inner_hbm, inner), (shared_hbm, shared)), small_done, 3)
    for copy in small:
        copy.wait()
    invert(reorder, place)
    for group in range(groups):
        seen[group] = 0
    moving = ids[device] - first
    dump = groups * stride

    def to_peer(slot, carry):
        peer = lax.div(place[first + slot], slots)
        rank = seen[peer]
        stays = slot != moving
        slot_of[jnp.where(stays, peer * stride + rank, dump)] = slot
        edge_place[slot] = peer * edge_block + rank
        seen[peer] = rank + stays.astype(jnp.int32)
        return carry

    lax.fori_loop(0, slots, to_peer, 0, unroll=4)
    peer = lax.div(place[dest[device]], slots)
    edge_place[moving] = peer * edge_block + seen[peer]
    peer = lax.div(place[first + moving], slots)
    slot_of[peer * stride + seen[peer]] = moving

    for read in reads:
        read.wait()
    writes = [pltpu.make_async_copy(staged.at[moving], leaving, write_done.at[0])]
    writes[-1].start()
    for step in range(1, groups):
        peer = peer_of(device, step, groups)
        for rank in range(early):
            slot = slot_of[peer * stride + rank]
            writes.append(pltpu.make_async_copy(staged.at[slot], out_early[step - 1].at[rank], write_done.at[0]))
            writes[-1].start()
    for peer in range(groups):
        slot = slot_of[peer * stride + stride - 1]
        writes.append(pltpu.make_async_copy(staged.at[slot], out_late.at[peer], write_done.at[0]))
        writes[-1].start()

    keep = inner.shape[0]
    rows = groups * edge_block
    lane = lax.broadcasted_iota(jnp.int32, (1, slots), 1)
    places = jnp.zeros((1, slots), jnp.int32)
    for slot in range(slots):
        places = jnp.where(lane == slot, edge_place[slot], places)
    row = lax.broadcasted_iota(jnp.int32, (rows, slots), 0)
    inner_sum = jnp.zeros((rows, inner.shape[2]), F32)
    shared_sum = jnp.zeros((rows, shared.shape[2]), F32)
    for copy in edges:
        copy.wait()
    for k in range(keep):
        pick = jnp.where(row == places + k * capacity, 1.0, 0.0).astype(BF16)
        inner_sum = inner_sum + jnp.dot(pick, inner[k], preferred_element_type=F32)
        shared_sum = shared_sum + jnp.dot(pick, shared[k], preferred_element_type=F32)
    packed = jnp.concatenate([inner_sum, shared_sum], axis=1).astype(BF16)
    lanes = out_edges.shape[2]
    for peer in range(groups):
        for block in range(packed.shape[1] // lanes):
            here = packed[peer * edge_block : (peer + 1) * edge_block, block * lanes : (block + 1) * lanes]
            out_edges[peer, block * edge_block : (block + 1) * edge_block, :] = here

    def from_origin(origin, carry):
        away = ids[origin]

        def one(slot, rank):
            old = origin * slots + slot
            new = place[old] - first
            mine = jnp.logical_and(jnp.logical_and(new >= 0, new < slots), old != away)
            new_slots[jnp.where(mine, origin * stride + rank, dump)] = new
            recv_rows[jnp.where(mine, new, slots)] = origin * edge_block + rank
            return rank + mine.astype(jnp.int32)

        rank = lax.fori_loop(0, slots, one, 0, unroll=8)
        kept[origin] = rank
        new = place[away] - first
        mine = jnp.logical_and(new >= 0, new < slots)
        new_slots[jnp.where(mine, origin * stride + rank, dump)] = new
        return carry

    lax.fori_loop(0, groups, from_origin, 0)

    def migrated(origin, carry):
        new = place[dest[origin]] - first
        mine = jnp.logical_and(new >= 0, new < slots)
        recv_rows[jnp.where(mine, new, slots)] = origin * edge_block + kept[origin]
        return carry

    lax.fori_loop(0, groups, migrated, 0)
    for write in writes:
        write.wait()


def pack(mig_ids, mig_dest, reorder, edge_inner, edge_shared, states, groups, early, capacity, edge_block):
    slots = states.shape[0]
    stride = slots // groups
    width = edge_inner.shape[2] + edge_shared.shape[2]
    lanes = states.shape[3]
    chunk = 8
    shape = jax.ShapeDtypeStruct
    peers = groups - 1 if early else 0
    inner = edge_inner.transpose(1, 0, 2)
    shared = edge_shared.transpose(1, 0, 2)
    return pl.pallas_call(
        functools.partial(pack_kernel, groups, slots, early, capacity, edge_block, chunk),
        out_shape=(
            shape((slots + 1,), jnp.int32),
            shape((slots + 1,), jnp.int32),
            shape((slots + 1,), jnp.int32),
            shape((groups, edge_block * width // lanes, lanes), BF16),
            shape(states.shape[1:], BF16),
            shape((groups,) + states.shape[1:], BF16),
        )
        + (shape((early,) + states.shape[1:], BF16),) * peers,
        in_specs=[HBM] * 6,
        out_specs=(SMEM, SMEM, SMEM, VMEM, HBM, HBM) + (HBM,) * peers,
        scratch_shapes=[
            pltpu.SMEM(mig_ids.shape, jnp.int32),
            pltpu.SMEM(mig_dest.shape, jnp.int32),
            pltpu.SMEM(reorder.shape, jnp.int32),
            pltpu.SMEM(reorder.shape, jnp.int32),
            pltpu.SMEM((slots,), jnp.int32),
            pltpu.SMEM((groups,), jnp.int32),
            pltpu.SMEM((groups,), jnp.int32),
            pltpu.VMEM(states.shape, states.dtype),
            pltpu.VMEM(inner.shape, BF16),
            pltpu.VMEM(shared.shape, BF16),
            pltpu.SemaphoreType.DMA((slots // chunk,)),
            pltpu.SemaphoreType.DMA((1,)),
            pltpu.SemaphoreType.DMA((5,)),
        ],
        compiler_params=pltpu.CompilerParams(vmem_limit_bytes=VMEM_BYTES),
        cost_estimate=CHEAP,
        name="pack",
    )(mig_ids, mig_dest, reorder, inner, shared, states)


def shift_rows(value, by):
    by = by % value.shape[0]
    return pltpu.roll(value, by, 0) if by else value


def mix(edge, fresh, weight, bias, token):
    taps = weight.shape[0]
    summed = fresh * weight[taps - 1 : taps] + bias
    for tap in range(taps - 1):
        back = taps - 1 - tap
        moved = jnp.where(token >= back, shift_rows(fresh, back), shift_rows(edge, -tap))
        summed = summed + moved * weight[tap : tap + 1]
    return summed / (1.0 + jnp.exp(-summed))


def latest(edge, fresh, counts, token, window):
    keep = window - 1
    result = edge
    for length in range(1, window + 1):
        chosen = jnp.where(token + length < keep, shift_rows(edge, -length), shift_rows(fresh, keep - length))
        result = jnp.where(counts == length, chosen, result)
    return result


def token_kernel(
    window,
    heads,
    head_dim,
    state_dim,
    capacity,
    skip_ref,
    recv_ref,
    rows_ref,
    shared_ref,
    edges_ref,
    counts_ref,
    conv_inner_ref,
    inner_bias_ref,
    conv_shared_ref,
    shared_bias_ref,
    step_bias_ref,
    decay_log_ref,
    moved_ref,
    entry_ref,
    readout_ref,
    within_ref,
    decay_ref,
    gate_ref,
    new_inner_ref,
    new_shared_ref,
):
    inner = heads * head_dim
    rows = rows_ref.shape[0]
    wide = lax.broadcasted_iota(jnp.int32, (rows, 1), 0)
    token = lax.rem(wide, window)
    counts = counts_ref[...]
    valid = token < counts

    arrived = edges_ref.shape[0]
    place = jnp.zeros((rows, 1), jnp.int32)
    for slot in range(rows // window):
        place = jnp.where(lax.div(wide, window) == slot, recv_ref[slot], place)
    pick = lax.broadcasted_iota(jnp.int32, (rows, arrived), 1) == place + token * capacity
    pick = jnp.logical_and(pick, token < window - 1)
    edges = jnp.dot(jnp.where(pick, 1.0, 0.0).astype(BF16), edges_ref[...], preferred_element_type=F32)

    gate = rows_ref[:, :inner].astype(F32)
    gate_ref[...] = jnp.where(valid, gate / (1.0 + jnp.exp(-gate)), 0.0)

    value = rows_ref[:, inner:].astype(F32)
    edge = edges[:, :inner]
    keep = window - 1
    slots = rows // window
    row = lax.broadcasted_iota(jnp.int32, (slots, rows), 0)
    lane = lax.broadcasted_iota(jnp.int32, (slots, rows), 1)
    takes = [jnp.where(lane == row * window + k, 1.0, 0.0).astype(BF16) for k in range(keep)]
    newest = latest(edge, value, counts, token, window).astype(BF16)
    for k in range(keep):
        new_inner_ref[k] = jnp.dot(takes[k], newest, preferred_element_type=F32).astype(BF16)
    mixed = mix(edge, value, conv_inner_ref[...], inner_bias_ref[...], token)

    fresh = shared_ref[:, : 2 * state_dim].astype(F32)
    edge = edges[:, inner:]
    newest = latest(edge, fresh, counts, token, window).astype(BF16)
    for k in range(keep):
        new_shared_ref[k] = jnp.dot(takes[k], newest, preferred_element_type=F32).astype(BF16)
    shared = mix(edge, fresh, conv_shared_ref[...], shared_bias_ref[...], token)
    entry = shared[:, :state_dim]
    readout = shared[:, state_dim:]
    entry_ref[...] = entry.astype(BF16)
    readout_t = readout.T.astype(BF16)
    readout_ref[...] = readout_t

    raw = shared_ref[:, 2 * state_dim :]
    all_heads = raw.shape[1]
    from_head = lax.broadcasted_iota(jnp.int32, (all_heads, rows), 0)
    to_lane = lax.broadcasted_iota(jnp.int32, (all_heads, rows), 1)
    pick = jnp.logical_and(from_head == to_lane + lax.axis_index("head") * heads, to_lane < heads)
    raw = jnp.dot(raw, pick.astype(BF16), preferred_element_type=F32) + step_bias_ref[...]
    step = jnp.maximum(raw, 0.0) + jnp.log(1.0 + jnp.exp(-jnp.abs(raw)))
    step = jnp.where(valid, step, 0.0)
    drop = step * -jnp.exp(decay_log_ref[...])
    total = drop
    after = drop
    reach = 1
    while reach < window:
        total = total + jnp.where(token >= reach, shift_rows(total, reach), 0.0)
        after = after + jnp.where(token + reach < window, shift_rows(after, -reach), 0.0)
        reach *= 2
    after = jnp.where(token + 1 < window, shift_rows(after, -1), 0.0)
    total_t = total.T
    decay_ref[...] = jnp.exp(total_t)[: decay_ref.shape[0]]
    carry_t = (step * jnp.exp(after)).T

    slot_a = lax.div(lax.broadcasted_iota(jnp.int32, (rows, rows), 0), window)
    slot_b = lax.div(lax.broadcasted_iota(jnp.int32, (rows, rows), 1), window)
    row_a = lax.broadcasted_iota(jnp.int32, (rows, rows), 0)
    row_b = lax.broadcasted_iota(jnp.int32, (rows, rows), 1)
    causal = jnp.logical_and(slot_a == slot_b, row_a <= row_b)
    overlap = jnp.dot(entry.astype(BF16), readout_t, preferred_element_type=F32)
    overlap = jnp.where(causal, overlap, 0.0)
    for block in range(inner // rows):
        turned = mixed[:, block * rows : (block + 1) * rows].T
        for part in range(rows // head_dim):
            head = block * (rows // head_dim) + part
            mine = turned[part * head_dim : (part + 1) * head_dim]
            here = pl.ds(head * head_dim, head_dim)
            moved_ref[here, :] = (mine * carry_t[head : head + 1]).astype(BF16)
            gap = jnp.minimum(total_t[head : head + 1] - total[:, head : head + 1], 0.0)
            weight = overlap * jnp.exp(gap) * step[:, head : head + 1]
            within_ref[here, :] = skip_ref[head] * mine + jnp.dot(
                mine.astype(BF16), weight.astype(BF16), preferred_element_type=F32
            )


def token_part(
    skip_gain, recv_rows, rows, shared, edges, counts, conv_inner, inner_bias, conv_shared, shared_bias, step_bias, decay_log, window, heads, head_dim, state_dim, capacity
):
    count = rows.shape[0]
    inner = heads * head_dim
    padded = -(-heads // 8) * 8
    shape = jax.ShapeDtypeStruct
    return pl.pallas_call(
        functools.partial(token_kernel, window, heads, head_dim, state_dim, capacity),
        out_shape=(
            shape((inner, count), BF16),
            shape((count, state_dim), BF16),
            shape((state_dim, count), BF16),
            shape((inner, count), F32),
            shape((padded, count), F32),
            shape((count, inner), F32),
            shape((window - 1, count // window, inner), BF16),
            shape((window - 1, count // window, 2 * state_dim), BF16),
        ),
        in_specs=[SMEM] * 2 + [VMEM] * 10,
        out_specs=(VMEM,) * 8,
        compiler_params=pltpu.CompilerParams(vmem_limit_bytes=VMEM_BYTES),
        cost_estimate=CHEAP,
        name="token_rows",
    )(skip_gain, recv_rows, rows, shared, edges, counts, conv_inner, inner_bias, conv_shared, shared_bias, step_bias, decay_log)


def page_jobs(groups, stride, steps, pages, late, states_ref, new_slots, slot_of):
    device = lax.axis_index("req")
    jobs = []
    pages = list(pages)
    for step in steps:
        origin = origin_of(device, step, groups)
        arrived = pages.pop(0) if step else None
        for rank in range(stride - 1):
            at = origin * stride + rank
            jobs.append((arrived.at[rank] if step else states_ref.at[slot_of[at]], new_slots[at]))
    if late is not None:
        jobs += [(late.at[origin], new_slots[origin * stride + stride - 1]) for origin in range(groups)]
    return jobs


def load_pages(jobs, batch, pages_in, read_done):
    return fetch([(source, pages_in.at[n]) for n, (source, _) in enumerate(jobs)], read_done)


def batches(jobs, batch):
    return [range(start, min(start + batch, len(jobs))) for start in range(0, len(jobs), batch)]


def read_pages(window, batch, jobs, loads, pages_in, readout):
    heads, head_dim, state_dim = pages_in.shape[1:]
    count = readout.shape[1]
    lane_slot = lax.div(lax.broadcasted_iota(jnp.int32, (state_dim, count), 1), window)
    total = None
    for group in batches(jobs, batch):
        for n in group:
            loads[n].wait()
        wanted = [jnp.where(lane_slot == jobs[n][1], readout[...], jnp.zeros((), BF16)) for n in group]
        held = jnp.concatenate([pages_in[n].reshape(heads * head_dim, state_dim) for n in group], axis=1)
        read = jnp.dot(held, jnp.concatenate(wanted, axis=0), preferred_element_type=F32)
        total = read if total is None else total + read
    return total


def update_pages(window, batch, jobs, loads, pages_in, pages_out, write_done, out_ref, moved, entry, decay):
    heads, head_dim, state_dim = pages_in.shape[1:]
    count = entry.shape[0]
    row_slot = lax.div(lax.broadcasted_iota(jnp.int32, (count, state_dim), 0), window)
    stores = []
    for group in batches(jobs, batch):
        for n in group if loads else ():
            loads[n].wait()
        entries = [jnp.where(row_slot == jobs[n][1], entry[...], jnp.zeros((), BF16)) for n in group]
        added = jnp.dot(moved[...], jnp.concatenate(entries, axis=1), preferred_element_type=F32)
        for q, n in enumerate(group):
            slot = jobs[n][1]
            lane = slot * window + window - 1
            for head in range(heads):
                here = slice(head * head_dim, (head + 1) * head_dim)
                kept = pages_in[n, head].astype(F32) * decay[head, lane]
                pages_out[n, head] = (kept + added[here, q * state_dim : (q + 1) * state_dim]).astype(BF16)
            stores.append(pltpu.make_async_copy(pages_out.at[n], out_ref.at[slot], write_done.at[0]))
            stores[-1].start()
    return stores


def early_kernel(window, batch, groups, stride, steps, new_slots, slot_of, decay_hbm, moved_hbm, entry_hbm, readout_hbm, states_ref, *refs):
    count = len([step for step in steps if step])
    out_ref, read_ref, moved, entry, readout, decay, pages_in, pages_out, read_done, write_done, small_done = refs[count:]
    pairs = ((decay_hbm, decay), (moved_hbm, moved), (entry_hbm, entry), (readout_hbm, readout))
    small = fetch(pairs, small_done)
    jobs = page_jobs(groups, stride, steps, refs[:count], None, states_ref, new_slots, slot_of)
    loads = load_pages(jobs, batch, pages_in, read_done)
    for copy in small:
        copy.wait()
    read_ref[...] = read_pages(window, batch, jobs, loads, pages_in, readout)
    for store in update_pages(window, batch, jobs, [], pages_in, pages_out, write_done, out_ref, moved, entry, decay):
        store.wait()


def hidden_kernel(
    window,
    batch,
    groups,
    stride,
    shares,
    steps,
    heads,
    head_dim,
    started,
    new_slots,
    decay_hbm,
    readout_hbm,
    within_hbm,
    gate_hbm,
    gain_hbm,
    weight_hbm,
    late,
    *refs,
):
    pages, refs = refs[: len(steps)], refs[len(steps) :]
    read_hbm = refs[0] if started else None
    refs = refs[1 if started else 0 :]
    messages, refs = refs[:shares], refs[shares:]
    readout, decay, within, gate, gain, weight, read, rows_all, pages_in, read_done, small_done = refs
    jobs = page_jobs(groups, stride, steps, pages, late, None, new_slots, None)
    pairs = [(readout_hbm, readout), (decay_hbm, decay), (within_hbm, within), (gate_hbm, gate), (gain_hbm, gain), (weight_hbm, weight)]
    small = fetch(pairs[:1], small_done)
    loads = load_pages(jobs, batch, pages_in, read_done)
    small += fetch(pairs[1:] + ([(read_hbm, read)] if started else []), small_done, 1)
    small[0].wait()
    total = read_pages(window, batch, jobs, loads, pages_in, readout)
    for copy in small[1:]:
        copy.wait()
    read[...] = total + read[...] if started else total
    count, inner = gate.shape
    factor = decay[...]
    blocks = []
    for block in range(inner // count):
        parts = []
        for part in range(count // head_dim):
            head = block * (count // head_dim) + part
            here = pl.ds(head * head_dim, head_dim)
            parts.append(read[here, :] * factor[head : head + 1] + within[here, :])
        blocks.append(jnp.concatenate(parts, axis=0).T)
    gated = jnp.concatenate(blocks, axis=1) * gate[...]
    squares = jnp.sum(gated * gated, axis=1, keepdims=True)
    high = squares.astype(BF16)
    low = (squares - high.astype(F32)).astype(BF16)
    scaled = (gated * gain[...]).astype(BF16)
    width = weight.shape[1]
    rows_all[:, :width] = jnp.dot(scaled, weight[...], preferred_element_type=F32).astype(BF16)
    lane = lax.broadcasted_iota(jnp.int32, (count, rows_all.shape[1] - width), 1)
    rows_all[:, width:] = jnp.where(lane == 0, high, jnp.where(lane == 1, low, jnp.zeros((), BF16)))
    own = count // shares
    for step in range(shares):
        start = peer_of(lax.axis_index("head"), step, shares) * own
        messages[step][...] = rows_all[pl.ds(pl.multiple_of(start, own), own), :]


def update_kernel(window, batch, groups, stride, steps, started, new_slots, decay_hbm, moved_hbm, entry_hbm, late, *refs):
    pages, refs = refs[: len(steps)], refs[len(steps) + (1 if started else 0) :]
    out_ref, moved, entry, decay, pages_in, pages_out, read_done, write_done, small_done = refs
    small = fetch(((decay_hbm, decay), (moved_hbm, moved), (entry_hbm, entry)), small_done)
    jobs = page_jobs(groups, stride, steps, pages, late, None, new_slots, None)
    loads = load_pages(jobs, batch, pages_in, read_done)
    for copy in small:
        copy.wait()
    for store in update_pages(window, batch, jobs, loads, pages_in, pages_out, write_done, out_ref, moved, entry, decay):
        store.wait()


def state_part(new_slots, slot_of, early_pages, steps, late, states, moved, entry, readout, within, decay, gate, gain, out_weight, window, groups, shares):
    slots, heads, head_dim, _ = states.shape
    page = states.shape[1:]
    stride = slots // groups
    count, inner = gate.shape
    width = out_weight.shape[1]
    shape = jax.ShapeDtypeStruct
    new_states = shape(states.shape, BF16)
    batch = 4
    rest = [step for step in early_pages if step not in steps]
    others = [early_pages[step] for step in rest]
    params = pltpu.CompilerParams(vmem_limit_bytes=VMEM_BYTES)

    def held(*arrays):
        return [pltpu.VMEM(array.shape, array.dtype) for array in arrays]

    def paging(jobs, copies):
        return [pltpu.VMEM((jobs,) + page, BF16)] * copies + [pltpu.SemaphoreType.DMA((jobs,))]

    done = pltpu.SemaphoreType.DMA
    decay_scalars = pltpu.SMEM(decay.shape, F32)
    read, begun = [], []
    if steps:
        arrived = [early_pages[step] for step in steps if step]
        operands = [new_slots, slot_of, decay, moved, entry, readout, states] + arrived
        out = pl.pallas_call(
            functools.partial(early_kernel, window, batch, groups, stride, steps),
            out_shape=(new_states, shape((inner, count), F32)),
            in_specs=[SMEM] * 2 + [HBM] * (len(operands) - 2),
            out_specs=(HBM, VMEM),
            scratch_shapes=held(moved, entry, readout) + [decay_scalars] + paging(len(steps) * (stride - 1), 2) + [done((1,)), done((4,))],
            compiler_params=params,
            cost_estimate=CHEAP,
            name="early_pages",
        )(*operands)
        begun, read = [out[0]], [out[1]]
    jobs = groups + len(rest) * (stride - 1)
    operands = [new_slots, decay, readout, within, gate, gain, out_weight, late] + others + read
    message = shape((count // shares, width + 128), BF16)
    messages = pl.pallas_call(
        functools.partial(hidden_kernel, window, batch, groups, stride, shares, rest, heads, head_dim, bool(read)),
        out_shape=(message,) * shares,
        in_specs=[SMEM] + [HBM] * (len(operands) - 1),
        out_specs=(VMEM,) * shares,
        scratch_shapes=held(readout, decay, within, gate, gain, out_weight, within)
        + [pltpu.VMEM((count, width + 128), BF16)]
        + paging(jobs, 1)
        + [done((7,))],
        compiler_params=params,
        cost_estimate=CHEAP,
        name="hidden_rows",
    )(*operands)
    operands = [new_slots, decay, moved, entry, late] + others + begun
    out = pl.pallas_call(
        functools.partial(update_kernel, window, batch, groups, stride, rest, bool(begun)),
        out_shape=new_states,
        in_specs=[SMEM] + [HBM] * (len(operands) - 1),
        out_specs=HBM,
        scratch_shapes=held(moved, entry) + [decay_scalars] + paging(jobs, 2) + [done((1,)), done((3,))],
        input_output_aliases={len(operands) - 1: 0} if begun else {},
        compiler_params=params,
        cost_estimate=pl.CostEstimate(flops=1, bytes_accessed=4 * states.size, transcendentals=0),
        name="late_pages",
    )(*operands)
    return out, messages


def local(
    tokens,
    pre_gain,
    inner_weight,
    shared_weight,
    conv_inner,
    conv_inner_bias,
    conv_shared,
    conv_shared_bias,
    step_bias,
    decay_log,
    skip_gain,
    gate_gain,
    out_weight,
    states,
    edge_inner,
    edge_shared,
    counts,
    mig_ids,
    mig_dest,
    reorder,
):
    slots, heads, head_dim, state_dim = states.shape
    inner = heads * head_dim
    groups = lax.axis_size("req")
    shares = lax.axis_size("head")
    request_index = lax.axis_index("req")
    head_index = lax.axis_index("head")
    own_rows = tokens.shape[0]
    window = own_rows * shares // slots
    width = tokens.shape[1]
    stride = slots // groups
    keep = edge_inner.shape[1]
    early = stride - 1
    capacity = stride + 1
    edge_block = -(-keep * capacity // 16) * 16
    exchange = functools.partial(lax.all_to_all, axis_name="req", split_axis=0, concat_axis=0, tiled=True)

    packed = pack(mig_ids, mig_dest, reorder, edge_inner, edge_shared, states, groups, early, capacity, edge_block)
    slot_of, recv_rows, new_slots, send_edges, page, send_late = packed[:6]
    early_pages = {step: permute(sent, "req", step) for step, sent in enumerate(packed[6:], 1)}
    first = list(range(2, groups, 2))[:2] if early_pages else []
    rest = [step for step in range(2, groups) if step not in first] if early_pages else []
    edge_rows = send_edges.shape[1]
    pieces = exchange(jnp.concatenate([send_edges, page.reshape(groups, inner // groups, state_dim)], axis=1))
    edges = pieces[:, :edge_rows].reshape(groups, -1, edge_block, state_dim).transpose(0, 2, 1, 3)
    edges = edges.reshape(groups * edge_block, -1)
    rows_in = tokens.astype(F32)
    normed = (rows_in * lax.rsqrt(jnp.mean(rows_in * rows_in, axis=-1, keepdims=True) + EPS) * pre_gain).astype(BF16)
    normed, pieces = lax.optimization_barrier((normed, pieces))
    all_rows = lax.all_to_all(jnp.tile(normed, (shares, 1)), "head", split_axis=0, concat_axis=0, tiled=True)
    comes_from = jnp.argmax(mig_dest[None, :] == mig_ids[:, None], axis=1)
    first_pages = [early_pages[step] for step in first]
    pieces, all_rows, first_pages = lax.optimization_barrier((pieces[comes_from, edge_rows:], all_rows, first_pages))
    early_pages.update(zip(first, first_pages))
    arrived = exchange(pieces).reshape(states.shape[1:])
    leaving = lax.dynamic_index_in_dim(mig_ids, request_index, 0, keepdims=False)
    target = jnp.argmax(reorder == leaving) // slots
    inner_flat = inner_weight.reshape(width, 2 * inner)
    inner_rows = jnp.dot(all_rows, inner_flat, preferred_element_type=F32).astype(BF16)
    shared_rows = jnp.dot(all_rows, shared_weight, preferred_element_type=F32).astype(BF16)

    lanes = slots * window

    def in_lanes(vector):
        return jnp.pad(vector, (0, lanes - heads)).reshape(1, lanes)

    moved, entry, readout, within, decay, gate, new_inner, new_shared = token_part(
        skip_gain,
        recv_rows,
        inner_rows,
        shared_rows,
        edges,
        jnp.repeat(counts, window).reshape(lanes, 1),
        conv_inner,
        conv_inner_bias.reshape(1, -1),
        conv_shared,
        conv_shared_bias.reshape(1, -1),
        in_lanes(step_bias),
        in_lanes(decay_log),
        window,
        heads,
        head_dim,
        state_dim,
        capacity,
    )
    send_late, _ = lax.optimization_barrier((send_late, [early_pages[step] for step in rest] + [moved]))
    late = exchange(lax.dynamic_update_index_in_dim(send_late, arrived, target, 0))
    edge_inner_out = new_inner.transpose(1, 0, 2)
    edge_shared_out = new_shared.transpose(1, 0, 2)

    states_out, messages = state_part(
        new_slots,
        slot_of,
        early_pages,
        list(range(groups)) if early_pages else [],
        late,
        states,
        moved,
        entry,
        readout,
        within,
        decay,
        gate,
        gate_gain.reshape(1, -1),
        out_weight,
        window,
        groups,
        shares,
    )
    total = jnp.zeros(messages[0].shape, F32)
    for step in range(shares):
        piece = permute(messages[step], "head", step) if step else messages[step]
        total = total + piece.astype(F32)
    squares = total[:, width : width + 1] + total[:, width + 1 : width + 2]
    mixer = total[:, :width] * lax.rsqrt(squares / (inner * shares) + EPS)
    hidden_out = (rows_in + mixer).astype(BF16)
    return (hidden_out, states_out, edge_inner_out, edge_shared_out)


def solution(mesh):
    placed = (
        P(("req", "head"), None),
        P(),
        P(None, None, "head"),
        P(),
        P(None, "head"),
        P("head"),
        P(),
        P(),
        P("head"),
        P("head"),
        P("head"),
        P("head"),
        P("head", None),
        P("req", "head", None, None),
        P("req", None, "head"),
        P("req", None, None),
        P("req"),
        P(),
        P(),
        P(),
    )
    return jax.shard_map(
        local,
        mesh=mesh,
        in_specs=placed,
        out_specs=(
            P(("req", "head"), None),
            P("req", "head", None, None),
            P("req", None, "head"),
            P("req", None, None),
        ),
        check_vma=False,
    )
```

```python
import functools

import jax
import jax.numpy as jnp
from jax import lax
from jax.experimental import pallas as pl
from jax.experimental.pallas import tpu as pltpu
from jax.sharding import PartitionSpec as P

EPS = 1e-05
F32 = jnp.float32
BF16 = jnp.bfloat16
VMEM_BYTES = 63 * 1024 * 1024
CHEAP = pl.CostEstimate(flops=1, bytes_accessed=1, transcendentals=0)
HBM = pl.BlockSpec(memory_space=pltpu.HBM)
SMEM = pl.BlockSpec(memory_space=pltpu.SMEM)
VMEM = pl.BlockSpec(memory_space=pltpu.VMEM)


def peer_of(index, step, size):
    if size & (size - 1) == 0:
        return index ^ step
    return lax.rem(index + step, size)


def origin_of(index, step, size):
    if size & (size - 1) == 0:
        return index ^ step
    return lax.rem(index - step + size, size)


def permute(value, axis, step):
    size = lax.axis_size(axis)
    pairs = [(i, i ^ step if size & (size - 1) == 0 else (i + step) % size) for i in range(size)]
    return lax.ppermute(value, axis, pairs)


def invert(order, place):
    def one(slot, carry):
        place[order[slot]] = slot
        return carry

    lax.fori_loop(0, order.shape[0], one, 0, unroll=16)


def fetch(pairs, done, first=0):
    copies = [pltpu.make_async_copy(source, target, done.at[first + n]) for n, (source, target) in enumerate(pairs)]
    for copy in copies:
        copy.start()
    return copies


def pack_kernel(
    groups,
    slots,
    early,
    capacity,
    edge_block,
    chunk,
    ids_hbm,
    dest_hbm,
    reorder_hbm,
    inner_hbm,
    shared_hbm,
    states_ref,
    slot_of,
    recv_rows,
    new_slots,
    out_edges,
    leaving,
    out_late,
    *refs,
):
    out_early = refs[: groups - 1] if early else []
    ids, dest, reorder, place, edge_place, seen, kept, staged, inner, shared, read_done, write_done, small_done = refs[len(out_early) :]
    stride = slots // groups
    device = lax.axis_index("req")
    first = device * slots
    small = fetch(((ids_hbm, ids), (dest_hbm, dest), (reorder_hbm, reorder)), small_done)
    parts = [pl.ds(part * chunk, chunk) for part in range(slots // chunk)]
    reads = fetch([(states_ref.at[part], staged.at[part]) for part in parts], read_done)
    edges = fetch(((inner_hbm, inner), (shared_hbm, shared)), small_done, 3)
    for copy in small:
        copy.wait()
    invert(reorder, place)
    for group in range(groups):
        seen[group] = 0
    moving = ids[device] - first
    dump = groups * stride

    def to_peer(slot, carry):
        peer = lax.div(place[first + slot], slots)
        rank = seen[peer]
        stays = slot != moving
        slot_of[jnp.where(stays, peer * stride + rank, dump)] = slot
        edge_place[slot] = peer * edge_block + rank
        seen[peer] = rank + stays.astype(jnp.int32)
        return carry

    lax.fori_loop(0, slots, to_peer, 0, unroll=4)
    peer = lax.div(place[dest[device]], slots)
    edge_place[moving] = peer * edge_block + seen[peer]
    peer = lax.div(place[first + moving], slots)
    slot_of[peer * stride + seen[peer]] = moving

    for read in reads:
        read.wait()
    writes = [pltpu.make_async_copy(staged.at[moving], leaving, write_done.at[0])]
    writes[-1].start()
    for step in range(1, groups):
        peer = peer_of(device, step, groups)
        for rank in range(early):
            slot = slot_of[peer * stride + rank]
            writes.append(pltpu.make_async_copy(staged.at[slot], out_early[step - 1].at[rank], write_done.at[0]))
            writes[-1].start()
    for peer in range(groups):
        slot = slot_of[peer * stride + stride - 1]
        writes.append(pltpu.make_async_copy(staged.at[slot], out_late.at[peer], write_done.at[0]))
        writes[-1].start()

    pieces = staged[moving].reshape(-1, staged.shape[3])
    edge_rows = edge_block * (inner.shape[2] + shared.shape[2]) // staged.shape[3]
    share = pieces.shape[0] // groups
    if out_edges.shape[1] > edge_rows:
        for peer in range(groups):
            out_edges[peer, edge_rows:, :] = pieces[peer * share : (peer + 1) * share]
    keep = inner.shape[0]
    rows = groups * edge_block
    lane = lax.broadcasted_iota(jnp.int32, (1, slots), 1)
    places = jnp.zeros((1, slots), jnp.int32)
    for slot in range(slots):
        places = jnp.where(lane == slot, edge_place[slot], places)
    row = lax.broadcasted_iota(jnp.int32, (rows, slots), 0)
    inner_sum = jnp.zeros((rows, inner.shape[2]), F32)
    shared_sum = jnp.zeros((rows, shared.shape[2]), F32)
    for copy in edges:
        copy.wait()
    for k in range(keep):
        pick = jnp.where(row == places + k * capacity, 1.0, 0.0).astype(BF16)
        inner_sum = inner_sum + jnp.dot(pick, inner[k], preferred_element_type=F32)
        shared_sum = shared_sum + jnp.dot(pick, shared[k], preferred_element_type=F32)
    packed = jnp.concatenate([inner_sum, shared_sum], axis=1).astype(BF16)
    lanes = out_edges.shape[2]
    for peer in range(groups):
        for block in range(packed.shape[1] // lanes):
            here = packed[peer * edge_block : (peer + 1) * edge_block, block * lanes : (block + 1) * lanes]
            out_edges[peer, block * edge_block : (block + 1) * edge_block, :] = here

    def from_origin(origin, carry):
        away = ids[origin]

        def one(slot, rank):
            old = origin * slots + slot
            new = place[old] - first
            mine = jnp.logical_and(jnp.logical_and(new >= 0, new < slots), old != away)
            new_slots[jnp.where(mine, origin * stride + rank, dump)] = new
            recv_rows[jnp.where(mine, new, slots)] = origin * edge_block + rank
            return rank + mine.astype(jnp.int32)

        rank = lax.fori_loop(0, slots, one, 0, unroll=8)
        kept[origin] = rank
        new = place[away] - first
        mine = jnp.logical_and(new >= 0, new < slots)
        new_slots[jnp.where(mine, origin * stride + rank, dump)] = new
        return carry

    lax.fori_loop(0, groups, from_origin, 0)

    def migrated(origin, carry):
        new = place[dest[origin]] - first
        mine = jnp.logical_and(new >= 0, new < slots)
        recv_rows[jnp.where(mine, new, slots)] = origin * edge_block + kept[origin]
        return carry

    lax.fori_loop(0, groups, migrated, 0)
    for write in writes:
        write.wait()


def pack(mig_ids, mig_dest, reorder, edge_inner, edge_shared, states, groups, early, capacity, edge_block):
    slots = states.shape[0]
    stride = slots // groups
    width = edge_inner.shape[2] + edge_shared.shape[2]
    lanes = states.shape[3]
    share = states.shape[1] * states.shape[2] // groups
    chunk = 8
    shape = jax.ShapeDtypeStruct
    peers = groups - 1 if early else 0
    inner = edge_inner.transpose(1, 0, 2)
    shared = edge_shared.transpose(1, 0, 2)
    return pl.pallas_call(
        functools.partial(pack_kernel, groups, slots, early, capacity, edge_block, chunk),
        out_shape=(
            shape((slots + 1,), jnp.int32),
            shape((slots + 1,), jnp.int32),
            shape((slots + 1,), jnp.int32),
            shape((groups, edge_block * width // lanes + (share if share % 16 == 0 else 0), lanes), BF16),
            shape(states.shape[1:], BF16),
            shape((groups,) + states.shape[1:], BF16),
        )
        + (shape((early,) + states.shape[1:], BF16),) * peers,
        in_specs=[HBM] * 6,
        out_specs=(SMEM, SMEM, SMEM, VMEM, HBM, HBM) + (HBM,) * peers,
        scratch_shapes=[
            pltpu.SMEM(mig_ids.shape, jnp.int32),
            pltpu.SMEM(mig_dest.shape, jnp.int32),
            pltpu.SMEM(reorder.shape, jnp.int32),
            pltpu.SMEM(reorder.shape, jnp.int32),
            pltpu.SMEM((slots,), jnp.int32),
            pltpu.SMEM((groups,), jnp.int32),
            pltpu.SMEM((groups,), jnp.int32),
            pltpu.VMEM(states.shape, states.dtype),
            pltpu.VMEM(inner.shape, BF16),
            pltpu.VMEM(shared.shape, BF16),
            pltpu.SemaphoreType.DMA((slots // chunk,)),
            pltpu.SemaphoreType.DMA((1,)),
            pltpu.SemaphoreType.DMA((5,)),
        ],
        compiler_params=pltpu.CompilerParams(vmem_limit_bytes=VMEM_BYTES),
        cost_estimate=CHEAP,
        name="pack",
    )(mig_ids, mig_dest, reorder, inner, shared, states)


def shift_rows(value, by):
    by = by % value.shape[0]
    return pltpu.roll(value, by, 0) if by else value


def mix(edge, fresh, weight, bias, token):
    taps = weight.shape[0]
    summed = fresh * weight[taps - 1 : taps] + bias
    for tap in range(taps - 1):
        back = taps - 1 - tap
        moved = jnp.where(token >= back, shift_rows(fresh, back), shift_rows(edge, -tap))
        summed = summed + moved * weight[tap : tap + 1]
    return summed / (1.0 + jnp.exp(-summed))


def latest(edge, fresh, counts, token, window):
    keep = window - 1
    result = edge
    for length in range(1, window + 1):
        chosen = jnp.where(token + length < keep, shift_rows(edge, -length), shift_rows(fresh, keep - length))
        result = jnp.where(counts == length, chosen, result)
    return result


def token_kernel(
    window,
    heads,
    head_dim,
    state_dim,
    capacity,
    skip_ref,
    recv_ref,
    rows_ref,
    shared_ref,
    edges_ref,
    counts_ref,
    conv_inner_ref,
    inner_bias_ref,
    conv_shared_ref,
    shared_bias_ref,
    step_bias_ref,
    decay_log_ref,
    moved_ref,
    entry_ref,
    readout_ref,
    within_ref,
    decay_ref,
    gate_ref,
    new_inner_ref,
    new_shared_ref,
):
    inner = heads * head_dim
    rows = rows_ref.shape[0]
    wide = lax.broadcasted_iota(jnp.int32, (rows, 1), 0)
    token = lax.rem(wide, window)
    counts = counts_ref[...]
    valid = token < counts

    arrived = edges_ref.shape[0]
    place = jnp.zeros((rows, 1), jnp.int32)
    for slot in range(rows // window):
        place = jnp.where(lax.div(wide, window) == slot, recv_ref[slot], place)
    pick = lax.broadcasted_iota(jnp.int32, (rows, arrived), 1) == place + token * capacity
    pick = jnp.logical_and(pick, token < window - 1)
    edges = jnp.dot(jnp.where(pick, 1.0, 0.0).astype(BF16), edges_ref[...], preferred_element_type=F32)

    gate = rows_ref[:, :inner].astype(F32)
    gate_ref[...] = jnp.where(valid, gate / (1.0 + jnp.exp(-gate)), 0.0)

    value = rows_ref[:, inner:].astype(F32)
    edge = edges[:, :inner]
    keep = window - 1
    slots = rows // window
    row = lax.broadcasted_iota(jnp.int32, (slots, rows), 0)
    lane = lax.broadcasted_iota(jnp.int32, (slots, rows), 1)
    takes = [jnp.where(lane == row * window + k, 1.0, 0.0).astype(BF16) for k in range(keep)]
    newest = latest(edge, value, counts, token, window).astype(BF16)
    for k in range(keep):
        new_inner_ref[k] = jnp.dot(takes[k], newest, preferred_element_type=F32).astype(BF16)
    mixed = mix(edge, value, conv_inner_ref[...], inner_bias_ref[...], token)

    fresh = shared_ref[:, : 2 * state_dim].astype(F32)
    edge = edges[:, inner:]
    newest = latest(edge, fresh, counts, token, window).astype(BF16)
    for k in range(keep):
        new_shared_ref[k] = jnp.dot(takes[k], newest, preferred_element_type=F32).astype(BF16)
    shared = mix(edge, fresh, conv_shared_ref[...], shared_bias_ref[...], token)
    entry = shared[:, :state_dim]
    readout = shared[:, state_dim:]
    entry_ref[...] = entry.astype(BF16)
    readout_t = readout.T.astype(BF16)
    readout_ref[...] = readout_t

    raw = shared_ref[:, 2 * state_dim :]
    all_heads = raw.shape[1]
    from_head = lax.broadcasted_iota(jnp.int32, (all_heads, rows), 0)
    to_lane = lax.broadcasted_iota(jnp.int32, (all_heads, rows), 1)
    pick = jnp.logical_and(from_head == to_lane + lax.axis_index("head") * heads, to_lane < heads)
    raw = jnp.dot(raw, pick.astype(BF16), preferred_element_type=F32) + step_bias_ref[...]
    step = jnp.maximum(raw, 0.0) + jnp.log(1.0 + jnp.exp(-jnp.abs(raw)))
    step = jnp.where(valid, step, 0.0)
    drop = step * -jnp.exp(decay_log_ref[...])
    total = drop
    after = drop
    reach = 1
    while reach < window:
        total = total + jnp.where(token >= reach, shift_rows(total, reach), 0.0)
        after = after + jnp.where(token + reach < window, shift_rows(after, -reach), 0.0)
        reach *= 2
    after = jnp.where(token + 1 < window, shift_rows(after, -1), 0.0)
    total_t = total.T
    decay_ref[...] = jnp.exp(total_t)[: decay_ref.shape[0]]
    carry_t = (step * jnp.exp(after)).T

    slot_a = lax.div(lax.broadcasted_iota(jnp.int32, (rows, rows), 0), window)
    slot_b = lax.div(lax.broadcasted_iota(jnp.int32, (rows, rows), 1), window)
    row_a = lax.broadcasted_iota(jnp.int32, (rows, rows), 0)
    row_b = lax.broadcasted_iota(jnp.int32, (rows, rows), 1)
    causal = jnp.logical_and(slot_a == slot_b, row_a <= row_b)
    overlap = jnp.dot(entry.astype(BF16), readout_t, preferred_element_type=F32)
    overlap = jnp.where(causal, overlap, 0.0)
    for block in range(inner // rows):
        turned = mixed[:, block * rows : (block + 1) * rows].T
        for part in range(rows // head_dim):
            head = block * (rows // head_dim) + part
            mine = turned[part * head_dim : (part + 1) * head_dim]
            here = pl.ds(head * head_dim, head_dim)
            moved_ref[here, :] = (mine * carry_t[head : head + 1]).astype(BF16)
            gap = jnp.minimum(total_t[head : head + 1] - total[:, head : head + 1], 0.0)
            weight = overlap * jnp.exp(gap) * step[:, head : head + 1]
            within_ref[here, :] = skip_ref[head] * mine + jnp.dot(
                mine.astype(BF16), weight.astype(BF16), preferred_element_type=F32
            )


def token_part(
    skip_gain, recv_rows, rows, shared, edges, counts, conv_inner, inner_bias, conv_shared, shared_bias, step_bias, decay_log, window, heads, head_dim, state_dim, capacity
):
    count = rows.shape[0]
    inner = heads * head_dim
    padded = -(-heads // 8) * 8
    shape = jax.ShapeDtypeStruct
    return pl.pallas_call(
        functools.partial(token_kernel, window, heads, head_dim, state_dim, capacity),
        out_shape=(
            shape((inner, count), BF16),
            shape((count, state_dim), BF16),
            shape((state_dim, count), BF16),
            shape((inner, count), F32),
            shape((padded, count), F32),
            shape((count, inner), F32),
            shape((window - 1, count // window, inner), BF16),
            shape((window - 1, count // window, 2 * state_dim), BF16),
        ),
        in_specs=[SMEM] * 2 + [VMEM] * 10,
        out_specs=(VMEM,) * 8,
        compiler_params=pltpu.CompilerParams(vmem_limit_bytes=VMEM_BYTES),
        cost_estimate=CHEAP,
        name="token_rows",
    )(skip_gain, recv_rows, rows, shared, edges, counts, conv_inner, inner_bias, conv_shared, shared_bias, step_bias, decay_log)


def page_jobs(groups, stride, steps, pages, late, states_ref, new_slots, slot_of):
    device = lax.axis_index("req")
    jobs = []
    pages = list(pages)
    for step in steps:
        origin = origin_of(device, step, groups)
        arrived = pages.pop(0) if step else None
        for rank in range(stride - 1):
            at = origin * stride + rank
            jobs.append((arrived.at[rank] if step else states_ref.at[slot_of[at]], new_slots[at]))
    if late is not None:
        jobs += [(late.at[origin], new_slots[origin * stride + stride - 1]) for origin in range(groups)]
    return jobs


def load_pages(jobs, batch, pages_in, read_done):
    return fetch([(source, pages_in.at[n]) for n, (source, _) in enumerate(jobs)], read_done)


def batches(jobs, batch):
    return [range(start, min(start + batch, len(jobs))) for start in range(0, len(jobs), batch)]


def read_pages(window, batch, jobs, loads, pages_in, readout):
    heads, head_dim, state_dim = pages_in.shape[1:]
    count = readout.shape[1]
    lane_slot = lax.div(lax.broadcasted_iota(jnp.int32, (state_dim, count), 1), window)
    total = None
    for group in batches(jobs, batch):
        for n in group:
            loads[n].wait()
        wanted = [jnp.where(lane_slot == jobs[n][1], readout[...], jnp.zeros((), BF16)) for n in group]
        held = jnp.concatenate([pages_in[n].reshape(heads * head_dim, state_dim) for n in group], axis=1)
        read = jnp.dot(held, jnp.concatenate(wanted, axis=0), preferred_element_type=F32)
        total = read if total is None else total + read
    return total


def update_pages(window, batch, jobs, loads, pages_in, pages_out, write_done, out_ref, moved, entry, decay):
    heads, head_dim, state_dim = pages_in.shape[1:]
    count = entry.shape[0]
    row_slot = lax.div(lax.broadcasted_iota(jnp.int32, (count, state_dim), 0), window)
    stores = []
    for group in batches(jobs, batch):
        for n in group if loads else ():
            loads[n].wait()
        entries = [jnp.where(row_slot == jobs[n][1], entry[...], jnp.zeros((), BF16)) for n in group]
        added = jnp.dot(moved[...], jnp.concatenate(entries, axis=1), preferred_element_type=F32)
        for q, n in enumerate(group):
            slot = jobs[n][1]
            lane = slot * window + window - 1
            for head in range(heads):
                here = slice(head * head_dim, (head + 1) * head_dim)
                kept = pages_in[n, head].astype(F32) * decay[head, lane]
                pages_out[n, head] = (kept + added[here, q * state_dim : (q + 1) * state_dim]).astype(BF16)
            stores.append(pltpu.make_async_copy(pages_out.at[n], out_ref.at[slot], write_done.at[0]))
            stores[-1].start()
    return stores


def early_kernel(window, batch, groups, stride, steps, new_slots, slot_of, decay_hbm, moved_hbm, entry_hbm, readout_hbm, states_ref, *refs):
    count = len([step for step in steps if step])
    out_ref, read_ref, moved, entry, readout, decay, pages_in, pages_out, read_done, write_done, small_done = refs[count:]
    pairs = ((decay_hbm, decay), (moved_hbm, moved), (entry_hbm, entry), (readout_hbm, readout))
    small = fetch(pairs, small_done)
    jobs = page_jobs(groups, stride, steps, refs[:count], None, states_ref, new_slots, slot_of)
    loads = load_pages(jobs, batch, pages_in, read_done)
    for copy in small:
        copy.wait()
    read_ref[...] = read_pages(window, batch, jobs, loads, pages_in, readout)
    for store in update_pages(window, batch, jobs, [], pages_in, pages_out, write_done, out_ref, moved, entry, decay):
        store.wait()


def hidden_kernel(
    window,
    batch,
    groups,
    stride,
    shares,
    steps,
    heads,
    head_dim,
    started,
    new_slots,
    decay_hbm,
    readout_hbm,
    within_hbm,
    gate_hbm,
    gain_hbm,
    weight_hbm,
    late,
    *refs,
):
    pages, refs = refs[: len(steps)], refs[len(steps) :]
    read_hbm = refs[0] if started else None
    refs = refs[1 if started else 0 :]
    messages, refs = refs[:shares], refs[shares:]
    readout, decay, within, gate, gain, weight, read, rows_all, pages_in, read_done, small_done = refs
    jobs = page_jobs(groups, stride, steps, pages, late, None, new_slots, None)
    pairs = [(readout_hbm, readout), (decay_hbm, decay), (within_hbm, within), (gate_hbm, gate), (gain_hbm, gain), (weight_hbm, weight)]
    small = fetch(pairs[:1], small_done)
    loads = load_pages(jobs, batch, pages_in, read_done)
    small += fetch(pairs[1:] + ([(read_hbm, read)] if started else []), small_done, 1)
    small[0].wait()
    total = read_pages(window, batch, jobs, loads, pages_in, readout)
    for copy in small[1:]:
        copy.wait()
    read[...] = total + read[...] if started else total
    count, inner = gate.shape
    factor = decay[...]
    blocks = []
    for block in range(inner // count):
        parts = []
        for part in range(count // head_dim):
            head = block * (count // head_dim) + part
            here = pl.ds(head * head_dim, head_dim)
            parts.append(read[here, :] * factor[head : head + 1] + within[here, :])
        blocks.append(jnp.concatenate(parts, axis=0).T)
    gated = jnp.concatenate(blocks, axis=1) * gate[...]
    squares = jnp.sum(gated * gated, axis=1, keepdims=True)
    high = squares.astype(BF16)
    low = (squares - high.astype(F32)).astype(BF16)
    scaled = (gated * gain[...]).astype(BF16)
    width = weight.shape[1]
    rows_all[:, :width] = jnp.dot(scaled, weight[...], preferred_element_type=F32).astype(BF16)
    lane = lax.broadcasted_iota(jnp.int32, (count, rows_all.shape[1] - width), 1)
    rows_all[:, width:] = jnp.where(lane == 0, high, jnp.where(lane == 1, low, jnp.zeros((), BF16)))
    own = count // shares
    for step in range(shares):
        start = peer_of(lax.axis_index("head"), step, shares) * own
        messages[step][...] = rows_all[pl.ds(pl.multiple_of(start, own), own), :]


def update_kernel(window, batch, groups, stride, steps, started, new_slots, decay_hbm, moved_hbm, entry_hbm, late, *refs):
    pages, refs = refs[: len(steps)], refs[len(steps) + (1 if started else 0) :]
    out_ref, moved, entry, decay, pages_in, pages_out, read_done, write_done, small_done = refs
    small = fetch(((decay_hbm, decay), (moved_hbm, moved), (entry_hbm, entry)), small_done)
    jobs = page_jobs(groups, stride, steps, pages, late, None, new_slots, None)
    loads = load_pages(jobs, batch, pages_in, read_done)
    for copy in small:
        copy.wait()
    for store in update_pages(window, batch, jobs, loads, pages_in, pages_out, write_done, out_ref, moved, entry, decay):
        store.wait()


def state_part(new_slots, slot_of, early_pages, steps, late, states, moved, entry, readout, within, decay, gate, gain, out_weight, window, groups, shares):
    slots, heads, head_dim, _ = states.shape
    page = states.shape[1:]
    stride = slots // groups
    count, inner = gate.shape
    width = out_weight.shape[1]
    shape = jax.ShapeDtypeStruct
    new_states = shape(states.shape, BF16)
    batch = 4
    floating = list(range(3, groups - 1, 2))
    rest = [step for step in early_pages if step not in steps]
    others = [early_pages[step] for step in rest]
    params = pltpu.CompilerParams(vmem_limit_bytes=VMEM_BYTES)

    def held(*arrays):
        return [pltpu.VMEM(array.shape, array.dtype) for array in arrays]

    def paging(jobs, copies):
        return [pltpu.VMEM((jobs,) + page, BF16)] * copies + [pltpu.SemaphoreType.DMA((jobs,))]

    done = pltpu.SemaphoreType.DMA
    decay_scalars = pltpu.SMEM(decay.shape, F32)
    read, begun = [], []
    if steps:
        arrived = [early_pages[step] for step in steps if step]
        operands = [new_slots, slot_of, decay, moved, entry, readout, states] + arrived
        out = pl.pallas_call(
            functools.partial(early_kernel, window, batch, groups, stride, steps),
            out_shape=(new_states, shape((inner, count), F32)),
            in_specs=[SMEM] * 2 + [HBM] * (len(operands) - 2),
            out_specs=(HBM, VMEM),
            scratch_shapes=held(moved, entry, readout) + [decay_scalars] + paging(len(steps) * (stride - 1), 2) + [done((1,)), done((4,))],
            compiler_params=params,
            cost_estimate=pl.CostEstimate(flops=12_000_000_000, bytes_accessed=1, transcendentals=0),
            name="early_pages",
        )(*operands)
        begun, read = [out[0]], [out[1]]
    jobs = groups + len(rest) * (stride - 1)
    operands = [new_slots, decay, readout, within, gate, gain, out_weight, late] + others + read
    message = shape((count // shares, width + 128), BF16)
    messages = pl.pallas_call(
        functools.partial(hidden_kernel, window, batch, groups, stride, shares, rest, heads, head_dim, bool(read)),
        out_shape=(message,) * shares,
        in_specs=[SMEM] + [HBM] * (len(operands) - 1),
        out_specs=(VMEM,) * shares,
        scratch_shapes=held(readout, decay, within, gate, gain, out_weight, within)
        + [pltpu.VMEM((count, width + 128), BF16)]
        + paging(jobs, 1)
        + [done((7,))],
        compiler_params=params,
        cost_estimate=CHEAP,
        name="hidden_rows",
    )(*operands)
    operands = [new_slots, decay, moved, entry, late] + others + begun
    out = pl.pallas_call(
        functools.partial(update_kernel, window, batch, groups, stride, rest, bool(begun)),
        out_shape=new_states,
        in_specs=[SMEM] + [HBM] * (len(operands) - 1),
        out_specs=HBM,
        scratch_shapes=held(moved, entry) + [decay_scalars] + paging(jobs, 2) + [done((1,)), done((3,))],
        input_output_aliases={len(operands) - 1: 0} if begun else {},
        compiler_params=params,
        cost_estimate=pl.CostEstimate(flops=1, bytes_accessed=4 * states.size, transcendentals=0),
        name="late_pages",
    )(*operands)
    return out, messages


def finish_kernel(full, tokens_hbm, *refs):
    count = (len(refs) - 3) // 2
    hbm, out_ref, tokens, held, done = refs[:count], refs[count], refs[count + 1], refs[count + 2 : -1], refs[-1]
    copies = fetch([(tokens_hbm, tokens)] + list(zip(hbm, held)), done)
    for copy in copies:
        copy.wait()
    total = held[0][...].astype(F32)
    for message in held[1:]:
        total = total + message[...].astype(F32)
    width = tokens.shape[1]
    squares = total[:, width : width + 1] + total[:, width + 1 : width + 2]
    mixer = total[:, :width] * lax.rsqrt(squares / full + EPS)
    out_ref[...] = (tokens[...].astype(F32) + mixer).astype(BF16)


def finish(tokens, messages, full):
    return pl.pallas_call(
        functools.partial(finish_kernel, full),
        out_shape=jax.ShapeDtypeStruct(tokens.shape, BF16),
        in_specs=[HBM] * (1 + len(messages)),
        out_specs=VMEM,
        scratch_shapes=[pltpu.VMEM(array.shape, BF16) for array in [tokens] + messages]
        + [pltpu.SemaphoreType.DMA((1 + len(messages),))],
        compiler_params=pltpu.CompilerParams(vmem_limit_bytes=VMEM_BYTES),
        cost_estimate=CHEAP,
        name="finish",
    )(tokens, *messages)


def local(
    tokens,
    pre_gain,
    inner_weight,
    shared_weight,
    conv_inner,
    conv_inner_bias,
    conv_shared,
    conv_shared_bias,
    step_bias,
    decay_log,
    skip_gain,
    gate_gain,
    out_weight,
    states,
    edge_inner,
    edge_shared,
    counts,
    mig_ids,
    mig_dest,
    reorder,
):
    slots, heads, head_dim, state_dim = states.shape
    inner = heads * head_dim
    groups = lax.axis_size("req")
    shares = lax.axis_size("head")
    request_index = lax.axis_index("req")
    head_index = lax.axis_index("head")
    own_rows = tokens.shape[0]
    window = own_rows * shares // slots
    width = tokens.shape[1]
    stride = slots // groups
    keep = edge_inner.shape[1]
    early = stride - 1
    capacity = stride + 1
    edge_block = -(-keep * capacity // 16) * 16
    exchange = functools.partial(lax.all_to_all, axis_name="req", split_axis=0, concat_axis=0, tiled=True)

    packed = pack(mig_ids, mig_dest, reorder, edge_inner, edge_shared, states, groups, early, capacity, edge_block)
    slot_of, recv_rows, new_slots, send_edges, page, send_late = packed[:6]
    sent = dict(enumerate(packed[6:], 1))
    behind = list(range(groups - 2, groups)) if len(sent) > 2 else []
    early_pages = {step: permute(sent[step], "req", step) for step in sent if step not in behind}
    first = list(range(2, groups, 2))[:2] if early_pages else []
    floating = list(range(3, groups - 1, 2))
    rest = [step for step in range(2, groups) if step not in first] if early_pages else []
    edge_rows = edge_block * (inner + 2 * state_dim) // state_dim
    if send_edges.shape[1] == edge_rows:
        send_edges = jnp.concatenate([send_edges, page.reshape(groups, inner // groups, state_dim)], axis=1)
    pieces = exchange(send_edges)
    edges = pieces[:, :edge_rows].reshape(groups, -1, edge_block, state_dim).transpose(0, 2, 1, 3)
    edges = edges.reshape(groups * edge_block, -1)
    rows_in = tokens.astype(F32)
    normed = (rows_in * lax.rsqrt(jnp.mean(rows_in * rows_in, axis=-1, keepdims=True) + EPS) * pre_gain).astype(BF16)
    comes_from = jnp.argmax(mig_dest[None, :] == mig_ids[:, None], axis=1)
    pieces = pieces[comes_from, edge_rows:]
    arrived = exchange(pieces)
    for step in behind:
        waiting, _ = lax.optimization_barrier((sent[step], arrived))
        early_pages[step] = permute(waiting, "req", step)
    arrived = arrived.reshape(states.shape[1:])
    all_rows = lax.all_gather(normed, "head", axis=0, tiled=True)
    all_rows, inner_weight, _ = lax.optimization_barrier((all_rows, inner_weight, pieces))
    leaving = lax.dynamic_index_in_dim(mig_ids, request_index, 0, keepdims=False)
    target = jnp.argmax(reorder == leaving) // slots
    inner_flat = inner_weight.reshape(width, 2 * inner)
    inner_rows = jnp.dot(all_rows, inner_flat, preferred_element_type=F32).astype(BF16)
    shared_rows = jnp.dot(all_rows, shared_weight, preferred_element_type=F32).astype(BF16)

    lanes = slots * window

    def in_lanes(vector):
        return jnp.pad(vector, (0, lanes - heads)).reshape(1, lanes)

    moved, entry, readout, within, decay, gate, new_inner, new_shared = token_part(
        skip_gain,
        recv_rows,
        inner_rows,
        shared_rows,
        edges,
        jnp.repeat(counts, window).reshape(lanes, 1),
        conv_inner,
        conv_inner_bias.reshape(1, -1),
        conv_shared,
        conv_shared_bias.reshape(1, -1),
        in_lanes(step_bias),
        in_lanes(decay_log),
        window,
        heads,
        head_dim,
        state_dim,
        capacity,
    )
    late = exchange(lax.dynamic_update_index_in_dim(send_late, arrived, target, 0))
    edge_inner_out = new_inner.transpose(1, 0, 2)
    edge_shared_out = new_shared.transpose(1, 0, 2)

    states_out, messages = state_part(
        new_slots,
        slot_of,
        early_pages,
        list(range(groups)) if sent else [],
        late,
        states,
        moved,
        entry,
        readout,
        within,
        decay,
        gate,
        gate_gain.reshape(1, -1),
        out_weight,
        window,
        groups,
        shares,
    )
    messages = [permute(message, "head", step) if step else message for step, message in enumerate(messages)]
    hidden_out = finish(tokens, messages, inner * shares)
    return (hidden_out, states_out, edge_inner_out, edge_shared_out)


def solution(mesh):
    placed = (
        P(("req", "head"), None),
        P(),
        P(None, None, "head"),
        P(),
        P(None, "head"),
        P("head"),
        P(),
        P(),
        P("head"),
        P("head"),
        P("head"),
        P("head"),
        P("head", None),
        P("req", "head", None, None),
        P("req", None, "head"),
        P("req", None, None),
        P("req"),
        P(),
        P(),
        P(),
    )
    return jax.shard_map(
        local,
        mesh=mesh,
        in_specs=placed,
        out_specs=(
            P(("req", "head"), None),
            P("req", "head", None, None),
            P("req", None, "head"),
            P("req", None, None),
        ),
        check_vma=False,
    )
```

```python
import functools

import jax
import jax.numpy as jnp
from jax import lax
from jax.experimental import pallas as pl
from jax.experimental.pallas import tpu as pltpu
from jax.sharding import PartitionSpec as P

EPS = 1e-05
F32 = jnp.float32
BF16 = jnp.bfloat16
VMEM_BYTES = 63 * 1024 * 1024
CHEAP = pl.CostEstimate(flops=1, bytes_accessed=1, transcendentals=0)
HBM = pl.BlockSpec(memory_space=pltpu.HBM)
SMEM = pl.BlockSpec(memory_space=pltpu.SMEM)
VMEM = pl.BlockSpec(memory_space=pltpu.VMEM)


def peer_of(index, step, size):
    if size & (size - 1) == 0:
        return index ^ step
    return lax.rem(index + step, size)


def origin_of(index, step, size):
    if size & (size - 1) == 0:
        return index ^ step
    return lax.rem(index - step + size, size)


def permute(value, axis, step):
    size = lax.axis_size(axis)
    pairs = [(i, i ^ step if size & (size - 1) == 0 else (i + step) % size) for i in range(size)]
    return lax.ppermute(value, axis, pairs)


def invert(order, place):
    def one(slot, carry):
        place[order[slot]] = slot
        return carry

    lax.fori_loop(0, order.shape[0], one, 0, unroll=16)


def fetch(pairs, done, first=0):
    copies = [pltpu.make_async_copy(source, target, done.at[first + n]) for n, (source, target) in enumerate(pairs)]
    for copy in copies:
        copy.start()
    return copies


def pack_kernel(
    groups,
    slots,
    early,
    capacity,
    edge_block,
    chunk,
    ids_hbm,
    dest_hbm,
    reorder_hbm,
    inner_hbm,
    shared_hbm,
    states_ref,
    slot_of,
    recv_rows,
    new_slots,
    out_edges,
    leaving,
    out_late,
    *refs,
):
    out_early = refs[: groups - 1] if early else []
    ids, dest, reorder, place, edge_place, seen, kept, staged, inner, shared, read_done, write_done, small_done = refs[len(out_early) :]
    stride = slots // groups
    device = lax.axis_index("req")
    first = device * slots
    small = fetch(((ids_hbm, ids), (dest_hbm, dest), (reorder_hbm, reorder)), small_done)
    parts = [pl.ds(part * chunk, chunk) for part in range(slots // chunk)]
    reads = fetch([(states_ref.at[part], staged.at[part]) for part in parts], read_done)
    edges = fetch(((inner_hbm, inner), (shared_hbm, shared)), small_done, 3)
    for copy in small:
        copy.wait()
    invert(reorder, place)
    for group in range(groups):
        seen[group] = 0
    moving = ids[device] - first
    dump = groups * stride

    def to_peer(slot, carry):
        peer = lax.div(place[first + slot], slots)
        rank = seen[peer]
        stays = slot != moving
        slot_of[jnp.where(stays, peer * stride + rank, dump)] = slot
        edge_place[slot] = peer * edge_block + rank
        seen[peer] = rank + stays.astype(jnp.int32)
        return carry

    lax.fori_loop(0, slots, to_peer, 0, unroll=4)
    peer = lax.div(place[dest[device]], slots)
    edge_place[moving] = peer * edge_block + seen[peer]
    peer = lax.div(place[first + moving], slots)
    slot_of[peer * stride + seen[peer]] = moving

    for read in reads:
        read.wait()
    writes = [pltpu.make_async_copy(staged.at[moving], leaving, write_done.at[0])]
    writes[-1].start()
    for step in range(1, groups):
        peer = peer_of(device, step, groups)
        for rank in range(early):
            slot = slot_of[peer * stride + rank]
            writes.append(pltpu.make_async_copy(staged.at[slot], out_early[step - 1].at[rank], write_done.at[0]))
            writes[-1].start()
    for peer in range(groups):
        slot = slot_of[peer * stride + stride - 1]
        writes.append(pltpu.make_async_copy(staged.at[slot], out_late.at[peer], write_done.at[0]))
        writes[-1].start()

    pieces = staged[moving].reshape(-1, staged.shape[3])
    edge_rows = edge_block * (inner.shape[2] + shared.shape[2]) // staged.shape[3]
    share = pieces.shape[0] // groups
    if out_edges.shape[1] > edge_rows:
        for peer in range(groups):
            out_edges[peer, edge_rows:, :] = pieces[peer * share : (peer + 1) * share]
    keep = inner.shape[0]
    rows = groups * edge_block
    lane = lax.broadcasted_iota(jnp.int32, (1, slots), 1)
    places = jnp.zeros((1, slots), jnp.int32)
    for slot in range(slots):
        places = jnp.where(lane == slot, edge_place[slot], places)
    row = lax.broadcasted_iota(jnp.int32, (rows, slots), 0)
    inner_sum = jnp.zeros((rows, inner.shape[2]), F32)
    shared_sum = jnp.zeros((rows, shared.shape[2]), F32)
    for copy in edges:
        copy.wait()
    for k in range(keep):
        pick = jnp.where(row == places + k * capacity, 1.0, 0.0).astype(BF16)
        inner_sum = inner_sum + jnp.dot(pick, inner[k], preferred_element_type=F32)
        shared_sum = shared_sum + jnp.dot(pick, shared[k], preferred_element_type=F32)
    packed = jnp.concatenate([inner_sum, shared_sum], axis=1).astype(BF16)
    lanes = out_edges.shape[2]
    for peer in range(groups):
        for block in range(packed.shape[1] // lanes):
            here = packed[peer * edge_block : (peer + 1) * edge_block, block * lanes : (block + 1) * lanes]
            out_edges[peer, block * edge_block : (block + 1) * edge_block, :] = here

    def from_origin(origin, carry):
        away = ids[origin]

        def one(slot, rank):
            old = origin * slots + slot
            new = place[old] - first
            mine = jnp.logical_and(jnp.logical_and(new >= 0, new < slots), old != away)
            new_slots[jnp.where(mine, origin * stride + rank, dump)] = new
            recv_rows[jnp.where(mine, new, slots)] = origin * edge_block + rank
            return rank + mine.astype(jnp.int32)

        rank = lax.fori_loop(0, slots, one, 0, unroll=8)
        kept[origin] = rank
        new = place[away] - first
        mine = jnp.logical_and(new >= 0, new < slots)
        new_slots[jnp.where(mine, origin * stride + rank, dump)] = new
        return carry

    lax.fori_loop(0, groups, from_origin, 0)

    def migrated(origin, carry):
        new = place[dest[origin]] - first
        mine = jnp.logical_and(new >= 0, new < slots)
        recv_rows[jnp.where(mine, new, slots)] = origin * edge_block + kept[origin]
        return carry

    lax.fori_loop(0, groups, migrated, 0)
    for write in writes:
        write.wait()


def pack(mig_ids, mig_dest, reorder, edge_inner, edge_shared, states, groups, early, capacity, edge_block):
    slots = states.shape[0]
    stride = slots // groups
    width = edge_inner.shape[2] + edge_shared.shape[2]
    lanes = states.shape[3]
    share = states.shape[1] * states.shape[2] // groups
    chunk = 8
    shape = jax.ShapeDtypeStruct
    peers = groups - 1 if early else 0
    inner = edge_inner.transpose(1, 0, 2)
    shared = edge_shared.transpose(1, 0, 2)
    return pl.pallas_call(
        functools.partial(pack_kernel, groups, slots, early, capacity, edge_block, chunk),
        out_shape=(
            shape((slots + 1,), jnp.int32),
            shape((slots + 1,), jnp.int32),
            shape((slots + 1,), jnp.int32),
            shape((groups, edge_block * width // lanes + (share if share % 16 == 0 else 0), lanes), BF16),
            shape(states.shape[1:], BF16),
            shape((groups,) + states.shape[1:], BF16),
        )
        + (shape((early,) + states.shape[1:], BF16),) * peers,
        in_specs=[HBM] * 6,
        out_specs=(SMEM, SMEM, SMEM, VMEM, HBM, HBM) + (HBM,) * peers,
        scratch_shapes=[
            pltpu.SMEM(mig_ids.shape, jnp.int32),
            pltpu.SMEM(mig_dest.shape, jnp.int32),
            pltpu.SMEM(reorder.shape, jnp.int32),
            pltpu.SMEM(reorder.shape, jnp.int32),
            pltpu.SMEM((slots,), jnp.int32),
            pltpu.SMEM((groups,), jnp.int32),
            pltpu.SMEM((groups,), jnp.int32),
            pltpu.VMEM(states.shape, states.dtype),
            pltpu.VMEM(inner.shape, BF16),
            pltpu.VMEM(shared.shape, BF16),
            pltpu.SemaphoreType.DMA((slots // chunk,)),
            pltpu.SemaphoreType.DMA((1,)),
            pltpu.SemaphoreType.DMA((5,)),
        ],
        compiler_params=pltpu.CompilerParams(vmem_limit_bytes=VMEM_BYTES),
        cost_estimate=CHEAP,
        name="pack",
    )(mig_ids, mig_dest, reorder, inner, shared, states)


def shift_rows(value, by):
    by = by % value.shape[0]
    return pltpu.roll(value, by, 0) if by else value


def mix(edge, fresh, weight, bias, token):
    taps = weight.shape[0]
    summed = fresh * weight[taps - 1 : taps] + bias
    for tap in range(taps - 1):
        back = taps - 1 - tap
        moved = jnp.where(token >= back, shift_rows(fresh, back), shift_rows(edge, -tap))
        summed = summed + moved * weight[tap : tap + 1]
    return summed / (1.0 + jnp.exp(-summed))


def latest(edge, fresh, counts, token, window):
    keep = window - 1
    result = edge
    for length in range(1, window + 1):
        chosen = jnp.where(token + length < keep, shift_rows(edge, -length), shift_rows(fresh, keep - length))
        result = jnp.where(counts == length, chosen, result)
    return result


def token_kernel(
    window,
    heads,
    head_dim,
    state_dim,
    capacity,
    skip_ref,
    recv_ref,
    rows_ref,
    shared_ref,
    edges_ref,
    counts_ref,
    conv_inner_ref,
    inner_bias_ref,
    conv_shared_ref,
    shared_bias_ref,
    step_bias_ref,
    decay_log_ref,
    moved_ref,
    entry_ref,
    readout_ref,
    within_ref,
    decay_ref,
    gate_ref,
    new_inner_ref,
    new_shared_ref,
):
    inner = heads * head_dim
    rows = rows_ref.shape[0]
    wide = lax.broadcasted_iota(jnp.int32, (rows, 1), 0)
    token = lax.rem(wide, window)
    counts = counts_ref[...]
    valid = token < counts

    arrived = edges_ref.shape[0]
    place = jnp.zeros((rows, 1), jnp.int32)
    for slot in range(rows // window):
        place = jnp.where(lax.div(wide, window) == slot, recv_ref[slot], place)
    pick = lax.broadcasted_iota(jnp.int32, (rows, arrived), 1) == place + token * capacity
    pick = jnp.logical_and(pick, token < window - 1)
    edges = jnp.dot(jnp.where(pick, 1.0, 0.0).astype(BF16), edges_ref[...], preferred_element_type=F32)

    gate = rows_ref[:, :inner].astype(F32)
    gate_ref[...] = jnp.where(valid, gate / (1.0 + jnp.exp(-gate)), 0.0)

    value = rows_ref[:, inner:].astype(F32)
    edge = edges[:, :inner]
    keep = window - 1
    slots = rows // window
    row = lax.broadcasted_iota(jnp.int32, (slots, rows), 0)
    lane = lax.broadcasted_iota(jnp.int32, (slots, rows), 1)
    takes = [jnp.where(lane == row * window + k, 1.0, 0.0).astype(BF16) for k in range(keep)]
    newest = latest(edge, value, counts, token, window).astype(BF16)
    for k in range(keep):
        new_inner_ref[k] = jnp.dot(takes[k], newest, preferred_element_type=F32).astype(BF16)
    mixed = mix(edge, value, conv_inner_ref[...], inner_bias_ref[...], token)

    fresh = shared_ref[:, : 2 * state_dim].astype(F32)
    edge = edges[:, inner:]
    newest = latest(edge, fresh, counts, token, window).astype(BF16)
    for k in range(keep):
        new_shared_ref[k] = jnp.dot(takes[k], newest, preferred_element_type=F32).astype(BF16)
    shared = mix(edge, fresh, conv_shared_ref[...], shared_bias_ref[...], token)
    entry = shared[:, :state_dim]
    readout = shared[:, state_dim:]
    entry_ref[...] = entry.astype(BF16)
    readout_t = readout.T.astype(BF16)
    readout_ref[...] = readout_t

    raw = shared_ref[:, 2 * state_dim :]
    all_heads = raw.shape[1]
    from_head = lax.broadcasted_iota(jnp.int32, (all_heads, rows), 0)
    to_lane = lax.broadcasted_iota(jnp.int32, (all_heads, rows), 1)
    pick = jnp.logical_and(from_head == to_lane + lax.axis_index("head") * heads, to_lane < heads)
    raw = jnp.dot(raw, pick.astype(BF16), preferred_element_type=F32) + step_bias_ref[...]
    step = jnp.maximum(raw, 0.0) + jnp.log(1.0 + jnp.exp(-jnp.abs(raw)))
    step = jnp.where(valid, step, 0.0)
    drop = step * -jnp.exp(decay_log_ref[...])
    total = drop
    after = drop
    reach = 1
    while reach < window:
        total = total + jnp.where(token >= reach, shift_rows(total, reach), 0.0)
        after = after + jnp.where(token + reach < window, shift_rows(after, -reach), 0.0)
        reach *= 2
    after = jnp.where(token + 1 < window, shift_rows(after, -1), 0.0)
    total_t = total.T
    decay_ref[...] = jnp.exp(total_t)[: decay_ref.shape[0]]
    carry_t = (step * jnp.exp(after)).T

    slot_a = lax.div(lax.broadcasted_iota(jnp.int32, (rows, rows), 0), window)
    slot_b = lax.div(lax.broadcasted_iota(jnp.int32, (rows, rows), 1), window)
    row_a = lax.broadcasted_iota(jnp.int32, (rows, rows), 0)
    row_b = lax.broadcasted_iota(jnp.int32, (rows, rows), 1)
    causal = jnp.logical_and(slot_a == slot_b, row_a <= row_b)
    overlap = jnp.dot(entry.astype(BF16), readout_t, preferred_element_type=F32)
    overlap = jnp.where(causal, overlap, 0.0)
    for block in range(inner // rows):
        turned = mixed[:, block * rows : (block + 1) * rows].T
        for part in range(rows // head_dim):
            head = block * (rows // head_dim) + part
            mine = turned[part * head_dim : (part + 1) * head_dim]
            here = pl.ds(head * head_dim, head_dim)
            moved_ref[here, :] = (mine * carry_t[head : head + 1]).astype(BF16)
            gap = jnp.minimum(total_t[head : head + 1] - total[:, head : head + 1], 0.0)
            weight = overlap * jnp.exp(gap) * step[:, head : head + 1]
            within_ref[here, :] = skip_ref[head] * mine + jnp.dot(
                mine.astype(BF16), weight.astype(BF16), preferred_element_type=F32
            )


def token_part(
    skip_gain, recv_rows, rows, shared, edges, counts, conv_inner, inner_bias, conv_shared, shared_bias, step_bias, decay_log, window, heads, head_dim, state_dim, capacity
):
    count = rows.shape[0]
    inner = heads * head_dim
    padded = -(-heads // 8) * 8
    shape = jax.ShapeDtypeStruct
    return pl.pallas_call(
        functools.partial(token_kernel, window, heads, head_dim, state_dim, capacity),
        out_shape=(
            shape((inner, count), BF16),
            shape((count, state_dim), BF16),
            shape((state_dim, count), BF16),
            shape((inner, count), F32),
            shape((padded, count), F32),
            shape((count, inner), F32),
            shape((window - 1, count // window, inner), BF16),
            shape((window - 1, count // window, 2 * state_dim), BF16),
        ),
        in_specs=[SMEM] * 2 + [VMEM] * 10,
        out_specs=(VMEM,) * 8,
        compiler_params=pltpu.CompilerParams(vmem_limit_bytes=VMEM_BYTES),
        cost_estimate=CHEAP,
        name="token_rows",
    )(skip_gain, recv_rows, rows, shared, edges, counts, conv_inner, inner_bias, conv_shared, shared_bias, step_bias, decay_log)


def page_jobs(groups, stride, steps, pages, late, states_ref, new_slots, slot_of):
    device = lax.axis_index("req")
    jobs = []
    pages = list(pages)
    for step in steps:
        origin = origin_of(device, step, groups)
        arrived = pages.pop(0) if step else None
        for rank in range(stride - 1):
            at = origin * stride + rank
            jobs.append((arrived.at[rank] if step else states_ref.at[slot_of[at]], new_slots[at]))
    if late is not None:
        jobs += [(late.at[origin], new_slots[origin * stride + stride - 1]) for origin in range(groups)]
    return jobs


def load_pages(jobs, batch, pages_in, read_done):
    return fetch([(source, pages_in.at[n]) for n, (source, _) in enumerate(jobs)], read_done)


def batches(jobs, batch):
    return [range(start, min(start + batch, len(jobs))) for start in range(0, len(jobs), batch)]


def read_pages(window, batch, jobs, loads, pages_in, readout):
    heads, head_dim, state_dim = pages_in.shape[1:]
    count = readout.shape[1]
    lane_slot = lax.div(lax.broadcasted_iota(jnp.int32, (state_dim, count), 1), window)
    total = None
    for group in batches(jobs, batch):
        for n in group:
            loads[n].wait()
        wanted = [jnp.where(lane_slot == jobs[n][1], readout[...], jnp.zeros((), BF16)) for n in group]
        held = jnp.concatenate([pages_in[n].reshape(heads * head_dim, state_dim) for n in group], axis=1)
        read = jnp.dot(held, jnp.concatenate(wanted, axis=0), preferred_element_type=F32)
        total = read if total is None else total + read
    return total


def update_pages(window, batch, jobs, loads, pages_in, pages_out, write_done, out_ref, moved, entry, decay):
    heads, head_dim, state_dim = pages_in.shape[1:]
    count = entry.shape[0]
    row_slot = lax.div(lax.broadcasted_iota(jnp.int32, (count, state_dim), 0), window)
    stores = []
    for group in batches(jobs, batch):
        for n in group if loads else ():
            loads[n].wait()
        entries = [jnp.where(row_slot == jobs[n][1], entry[...], jnp.zeros((), BF16)) for n in group]
        added = jnp.dot(moved[...], jnp.concatenate(entries, axis=1), preferred_element_type=F32)
        for q, n in enumerate(group):
            slot = jobs[n][1]
            lane = slot * window + window - 1
            for head in range(heads):
                here = slice(head * head_dim, (head + 1) * head_dim)
                kept = pages_in[n, head].astype(F32) * decay[head, lane]
                pages_out[n, head] = (kept + added[here, q * state_dim : (q + 1) * state_dim]).astype(BF16)
            stores.append(pltpu.make_async_copy(pages_out.at[n], out_ref.at[slot], write_done.at[0]))
            stores[-1].start()
    return stores


def early_kernel(window, batch, groups, stride, steps, new_slots, slot_of, decay_hbm, moved_hbm, entry_hbm, readout_hbm, states_ref, *refs):
    count = len([step for step in steps if step])
    out_ref, read_ref, moved, entry, readout, decay, pages_in, pages_out, read_done, write_done, small_done = refs[count:]
    pairs = ((decay_hbm, decay), (moved_hbm, moved), (entry_hbm, entry), (readout_hbm, readout))
    small = fetch(pairs, small_done)
    jobs = page_jobs(groups, stride, steps, refs[:count], None, states_ref, new_slots, slot_of)
    loads = load_pages(jobs, batch, pages_in, read_done)
    for copy in small:
        copy.wait()
    read_ref[...] = read_pages(window, batch, jobs, loads, pages_in, readout)
    for store in update_pages(window, batch, jobs, [], pages_in, pages_out, write_done, out_ref, moved, entry, decay):
        store.wait()


def hidden_kernel(
    window,
    batch,
    groups,
    stride,
    shares,
    steps,
    heads,
    head_dim,
    started,
    new_slots,
    decay_hbm,
    readout_hbm,
    within_hbm,
    gate_hbm,
    gain_hbm,
    weight_hbm,
    late,
    *refs,
):
    pages, refs = refs[: len(steps)], refs[len(steps) :]
    read_hbm = refs[0] if started else None
    refs = refs[1 if started else 0 :]
    messages, refs = refs[:shares], refs[shares:]
    readout, decay, within, gate, gain, weight, read, rows_all, pages_in, read_done, small_done = refs
    jobs = page_jobs(groups, stride, steps, pages, late, None, new_slots, None)
    pairs = [(readout_hbm, readout), (decay_hbm, decay), (within_hbm, within), (gate_hbm, gate), (gain_hbm, gain), (weight_hbm, weight)]
    small = fetch(pairs[:1], small_done)
    loads = load_pages(jobs, batch, pages_in, read_done)
    small += fetch(pairs[1:] + ([(read_hbm, read)] if started else []), small_done, 1)
    small[0].wait()
    total = read_pages(window, batch, jobs, loads, pages_in, readout)
    for copy in small[1:]:
        copy.wait()
    read[...] = total + read[...] if started else total
    count, inner = gate.shape
    factor = decay[...]
    blocks = []
    for block in range(inner // count):
        parts = []
        for part in range(count // head_dim):
            head = block * (count // head_dim) + part
            here = pl.ds(head * head_dim, head_dim)
            parts.append(read[here, :] * factor[head : head + 1] + within[here, :])
        blocks.append(jnp.concatenate(parts, axis=0).T)
    gated = jnp.concatenate(blocks, axis=1) * gate[...]
    squares = jnp.sum(gated * gated, axis=1, keepdims=True)
    high = squares.astype(BF16)
    low = (squares - high.astype(F32)).astype(BF16)
    scaled = (gated * gain[...]).astype(BF16)
    width = weight.shape[1]
    rows_all[:, :width] = jnp.dot(scaled, weight[...], preferred_element_type=F32).astype(BF16)
    lane = lax.broadcasted_iota(jnp.int32, (count, rows_all.shape[1] - width), 1)
    rows_all[:, width:] = jnp.where(lane == 0, high, jnp.where(lane == 1, low, jnp.zeros((), BF16)))
    own = count // shares
    for step in range(shares):
        start = peer_of(lax.axis_index("head"), step, shares) * own
        messages[step][...] = rows_all[pl.ds(pl.multiple_of(start, own), own), :]


def update_kernel(window, batch, groups, stride, steps, started, new_slots, decay_hbm, moved_hbm, entry_hbm, late, *refs):
    pages, refs = refs[: len(steps)], refs[len(steps) + (1 if started else 0) :]
    out_ref, moved, entry, decay, pages_in, pages_out, read_done, write_done, small_done = refs
    small = fetch(((decay_hbm, decay), (moved_hbm, moved), (entry_hbm, entry)), small_done)
    jobs = page_jobs(groups, stride, steps, pages, late, None, new_slots, None)
    loads = load_pages(jobs, batch, pages_in, read_done)
    for copy in small:
        copy.wait()
    for store in update_pages(window, batch, jobs, loads, pages_in, pages_out, write_done, out_ref, moved, entry, decay):
        store.wait()


def state_part(new_slots, slot_of, early_pages, steps, late, states, moved, entry, readout, within, decay, gate, gain, out_weight, window, groups, shares):
    slots, heads, head_dim, _ = states.shape
    page = states.shape[1:]
    stride = slots // groups
    count, inner = gate.shape
    width = out_weight.shape[1]
    shape = jax.ShapeDtypeStruct
    new_states = shape(states.shape, BF16)
    batch = 4
    floating = list(range(3, groups - 1, 2))
    rest = [step for step in early_pages if step not in steps]
    others = [early_pages[step] for step in rest]
    params = pltpu.CompilerParams(vmem_limit_bytes=VMEM_BYTES)

    def held(*arrays):
        return [pltpu.VMEM(array.shape, array.dtype) for array in arrays]

    def paging(jobs, copies):
        return [pltpu.VMEM((jobs,) + page, BF16)] * copies + [pltpu.SemaphoreType.DMA((jobs,))]

    done = pltpu.SemaphoreType.DMA
    decay_scalars = pltpu.SMEM(decay.shape, F32)
    read, begun = [], []
    if steps:
        arrived = [early_pages[step] for step in steps if step]
        operands = [new_slots, slot_of, decay, moved, entry, readout, states] + arrived
        out = pl.pallas_call(
            functools.partial(early_kernel, window, batch, groups, stride, steps),
            out_shape=(new_states, shape((inner, count), F32)),
            in_specs=[SMEM] * 2 + [HBM] * (len(operands) - 2),
            out_specs=(HBM, VMEM),
            scratch_shapes=held(moved, entry, readout) + [decay_scalars] + paging(len(steps) * (stride - 1), 2) + [done((1,)), done((4,))],
            compiler_params=params,
            cost_estimate=pl.CostEstimate(flops=12_000_000_000, bytes_accessed=1, transcendentals=0),
            name="early_pages",
        )(*operands)
        begun, read = [out[0]], [out[1]]
    jobs = groups + len(rest) * (stride - 1)
    operands = [new_slots, decay, readout, within, gate, gain, out_weight, late] + others + read
    message = shape((count // shares, width + 128), BF16)
    messages = pl.pallas_call(
        functools.partial(hidden_kernel, window, batch, groups, stride, shares, rest, heads, head_dim, bool(read)),
        out_shape=(message,) * shares,
        in_specs=[SMEM] + [HBM] * (len(operands) - 1),
        out_specs=(VMEM,) * shares,
        scratch_shapes=held(readout, decay, within, gate, gain, out_weight, within)
        + [pltpu.VMEM((count, width + 128), BF16)]
        + paging(jobs, 1)
        + [done((7,))],
        compiler_params=params,
        cost_estimate=CHEAP,
        name="hidden_rows",
    )(*operands)
    operands = [new_slots, decay, moved, entry, late] + others + begun
    out = pl.pallas_call(
        functools.partial(update_kernel, window, batch, groups, stride, rest, bool(begun)),
        out_shape=new_states,
        in_specs=[SMEM] + [HBM] * (len(operands) - 1),
        out_specs=HBM,
        scratch_shapes=held(moved, entry) + [decay_scalars] + paging(jobs, 2) + [done((1,)), done((3,))],
        input_output_aliases={len(operands) - 1: 0} if begun else {},
        compiler_params=params,
        cost_estimate=pl.CostEstimate(flops=1, bytes_accessed=4 * states.size, transcendentals=0),
        name="late_pages",
    )(*operands)
    return out, messages


def finish_kernel(full, tokens_hbm, *refs):
    count = (len(refs) - 3) // 2
    hbm, out_ref, tokens, held, done = refs[:count], refs[count], refs[count + 1], refs[count + 2 : -1], refs[-1]
    copies = fetch([(tokens_hbm, tokens)] + list(zip(hbm, held)), done)
    for copy in copies:
        copy.wait()
    total = held[0][...].astype(F32)
    for message in held[1:]:
        total = total + message[...].astype(F32)
    width = tokens.shape[1]
    squares = total[:, width : width + 1] + total[:, width + 1 : width + 2]
    mixer = total[:, :width] * lax.rsqrt(squares / full + EPS)
    out_ref[...] = (tokens[...].astype(F32) + mixer).astype(BF16)


def finish(tokens, messages, full):
    return pl.pallas_call(
        functools.partial(finish_kernel, full),
        out_shape=jax.ShapeDtypeStruct(tokens.shape, BF16),
        in_specs=[HBM] * (1 + len(messages)),
        out_specs=VMEM,
        scratch_shapes=[pltpu.VMEM(array.shape, BF16) for array in [tokens] + messages]
        + [pltpu.SemaphoreType.DMA((1 + len(messages),))],
        compiler_params=pltpu.CompilerParams(vmem_limit_bytes=VMEM_BYTES),
        cost_estimate=CHEAP,
        name="finish",
    )(tokens, *messages)


def local(
    tokens,
    pre_gain,
    inner_weight,
    shared_weight,
    conv_inner,
    conv_inner_bias,
    conv_shared,
    conv_shared_bias,
    step_bias,
    decay_log,
    skip_gain,
    gate_gain,
    out_weight,
    states,
    edge_inner,
    edge_shared,
    counts,
    mig_ids,
    mig_dest,
    reorder,
):
    slots, heads, head_dim, state_dim = states.shape
    inner = heads * head_dim
    groups = lax.axis_size("req")
    shares = lax.axis_size("head")
    request_index = lax.axis_index("req")
    head_index = lax.axis_index("head")
    own_rows = tokens.shape[0]
    window = own_rows * shares // slots
    width = tokens.shape[1]
    stride = slots // groups
    keep = edge_inner.shape[1]
    early = stride - 1
    capacity = stride + 1
    edge_block = -(-keep * capacity // 16) * 16
    exchange = functools.partial(lax.all_to_all, axis_name="req", split_axis=0, concat_axis=0, tiled=True)

    packed = pack(mig_ids, mig_dest, reorder, edge_inner, edge_shared, states, groups, early, capacity, edge_block)
    slot_of, recv_rows, new_slots, send_edges, page, send_late = packed[:6]
    sent = dict(enumerate(packed[6:], 1))
    behind = [1, groups - 2, groups - 1] if len(sent) > 2 else []
    early_pages = {step: permute(sent[step], "req", step) for step in sent if step not in behind}
    first = list(range(2, groups, 2))[:2] if early_pages else []
    floating = list(range(3, groups - 1, 2))
    rest = [step for step in range(2, groups) if step not in first] if early_pages else []
    edge_rows = edge_block * (inner + 2 * state_dim) // state_dim
    if send_edges.shape[1] == edge_rows:
        send_edges = jnp.concatenate([send_edges, page.reshape(groups, inner // groups, state_dim)], axis=1)
    pieces = exchange(send_edges)
    edges = pieces[:, :edge_rows].reshape(groups, -1, edge_block, state_dim).transpose(0, 2, 1, 3)
    edges = edges.reshape(groups * edge_block, -1)
    rows_in = tokens.astype(F32)
    normed = (rows_in * lax.rsqrt(jnp.mean(rows_in * rows_in, axis=-1, keepdims=True) + EPS) * pre_gain).astype(BF16)
    comes_from = jnp.argmax(mig_dest[None, :] == mig_ids[:, None], axis=1)
    pieces = pieces[comes_from, edge_rows:]
    arrived = exchange(pieces)
    for step in behind:
        waiting, _ = lax.optimization_barrier((sent[step], pieces if step == groups - 2 else arrived))
        early_pages[step] = permute(waiting, "req", step)
    arrived = arrived.reshape(states.shape[1:])
    all_rows = lax.all_gather(normed, "head", axis=0, tiled=True)
    all_rows, inner_weight, _ = lax.optimization_barrier((all_rows, inner_weight, pieces))
    leaving = lax.dynamic_index_in_dim(mig_ids, request_index, 0, keepdims=False)
    target = jnp.argmax(reorder == leaving) // slots
    inner_flat = inner_weight.reshape(width, 2 * inner)
    inner_rows = jnp.dot(all_rows, inner_flat, preferred_element_type=F32).astype(BF16)
    shared_rows = jnp.dot(all_rows, shared_weight, preferred_element_type=F32).astype(BF16)

    lanes = slots * window

    def in_lanes(vector):
        return jnp.pad(vector, (0, lanes - heads)).reshape(1, lanes)

    moved, entry, readout, within, decay, gate, new_inner, new_shared = token_part(
        skip_gain,
        recv_rows,
        inner_rows,
        shared_rows,
        edges,
        jnp.repeat(counts, window).reshape(lanes, 1),
        conv_inner,
        conv_inner_bias.reshape(1, -1),
        conv_shared,
        conv_shared_bias.reshape(1, -1),
        in_lanes(step_bias),
        in_lanes(decay_log),
        window,
        heads,
        head_dim,
        state_dim,
        capacity,
    )
    late = exchange(lax.dynamic_update_index_in_dim(send_late, arrived, target, 0))
    edge_inner_out = new_inner.transpose(1, 0, 2)
    edge_shared_out = new_shared.transpose(1, 0, 2)

    states_out, messages = state_part(
        new_slots,
        slot_of,
        early_pages,
        list(range(groups)) if sent else [],
        late,
        states,
        moved,
        entry,
        readout,
        within,
        decay,
        gate,
        gate_gain.reshape(1, -1),
        out_weight,
        window,
        groups,
        shares,
    )
    messages = [permute(message, "head", step) if step else message for step, message in enumerate(messages)]
    hidden_out = finish(tokens, messages, inner * shares)
    return (hidden_out, states_out, edge_inner_out, edge_shared_out)


def solution(mesh):
    placed = (
        P(("req", "head"), None),
        P(),
        P(None, None, "head"),
        P(),
        P(None, "head"),
        P("head"),
        P(),
        P(),
        P("head"),
        P("head"),
        P("head"),
        P("head"),
        P("head", None),
        P("req", "head", None, None),
        P("req", None, "head"),
        P("req", None, None),
        P("req"),
        P(),
        P(),
        P(),
    )
    return jax.shard_map(
        local,
        mesh=mesh,
        in_specs=placed,
        out_specs=(
            P(("req", "head"), None),
            P("req", "head", None, None),
            P("req", None, "head"),
            P("req", None, None),
        ),
        check_vma=False,
    )
```

```python
import functools

import jax
import jax.numpy as jnp
from jax import lax
from jax.experimental import pallas as pl
from jax.experimental.pallas import tpu as pltpu
from jax.sharding import PartitionSpec as P

EPS = 1e-05
F32 = jnp.float32
BF16 = jnp.bfloat16
VMEM_BYTES = 63 * 1024 * 1024
CHEAP = pl.CostEstimate(flops=1, bytes_accessed=1, transcendentals=0)
HBM = pl.BlockSpec(memory_space=pltpu.HBM)
SMEM = pl.BlockSpec(memory_space=pltpu.SMEM)
VMEM = pl.BlockSpec(memory_space=pltpu.VMEM)


def peer_of(index, step, size):
    if size & (size - 1) == 0:
        return index ^ step
    return lax.rem(index + step, size)


def origin_of(index, step, size):
    if size & (size - 1) == 0:
        return index ^ step
    return lax.rem(index - step + size, size)


def permute(value, axis, step):
    size = lax.axis_size(axis)
    pairs = [(i, i ^ step if size & (size - 1) == 0 else (i + step) % size) for i in range(size)]
    return lax.ppermute(value, axis, pairs)


def invert(order, place):
    def one(slot, carry):
        place[order[slot]] = slot
        return carry

    lax.fori_loop(0, order.shape[0], one, 0, unroll=16)


def fetch(pairs, done, first=0):
    copies = [pltpu.make_async_copy(source, target, done.at[first + n]) for n, (source, target) in enumerate(pairs)]
    for copy in copies:
        copy.start()
    return copies


def pack_kernel(
    groups,
    slots,
    early,
    capacity,
    edge_block,
    chunk,
    ids_hbm,
    dest_hbm,
    reorder_hbm,
    inner_hbm,
    shared_hbm,
    states_ref,
    slot_of,
    recv_rows,
    new_slots,
    out_edges,
    leaving,
    out_late,
    *refs,
):
    out_early = refs[: groups - 1] if early else []
    ids, dest, reorder, place, edge_place, seen, kept, staged, inner, shared, read_done, write_done, small_done = refs[len(out_early) :]
    stride = slots // groups
    device = lax.axis_index("req")
    first = device * slots
    small = fetch(((ids_hbm, ids), (dest_hbm, dest), (reorder_hbm, reorder)), small_done)
    parts = [pl.ds(part * chunk, chunk) for part in range(slots // chunk)]
    reads = fetch([(states_ref.at[part], staged.at[part]) for part in parts], read_done)
    edges = fetch(((inner_hbm, inner), (shared_hbm, shared)), small_done, 3)
    for copy in small:
        copy.wait()
    invert(reorder, place)
    for group in range(groups):
        seen[group] = 0
    moving = ids[device] - first
    dump = groups * stride

    def to_peer(slot, carry):
        peer = lax.div(place[first + slot], slots)
        rank = seen[peer]
        stays = slot != moving
        slot_of[jnp.where(stays, peer * stride + rank, dump)] = slot
        edge_place[slot] = peer * edge_block + rank
        seen[peer] = rank + stays.astype(jnp.int32)
        return carry

    lax.fori_loop(0, slots, to_peer, 0, unroll=4)
    peer = lax.div(place[dest[device]], slots)
    edge_place[moving] = peer * edge_block + seen[peer]
    peer = lax.div(place[first + moving], slots)
    slot_of[peer * stride + seen[peer]] = moving

    jobs = [(moving, leaving)]
    for step in range(1, groups):
        peer = peer_of(device, step, groups)
        jobs += [(slot_of[peer * stride + rank], out_early[step - 1].at[rank]) for rank in range(early)]
    jobs += [(slot_of[peer * stride + stride - 1], out_late.at[peer]) for peer in range(groups)]
    writes = [pltpu.make_async_copy(staged.at[slot], target, write_done.at[0]) for slot, target in jobs]
    half = len(reads) // 2
    for lower in (True, False):
        for read in reads[:half] if lower else reads[half:]:
            read.wait()
        for (slot, _), write in zip(jobs, writes):
            pl.when((slot < half * chunk) == lower)(write.start)

    pieces = staged[moving].reshape(-1, staged.shape[3])
    edge_rows = edge_block * (inner.shape[2] + shared.shape[2]) // staged.shape[3]
    share = pieces.shape[0] // groups
    if out_edges.shape[1] > edge_rows:
        for peer in range(groups):
            out_edges[peer, edge_rows:, :] = pieces[peer * share : (peer + 1) * share]
    keep = inner.shape[0]
    rows = groups * edge_block
    lane = lax.broadcasted_iota(jnp.int32, (1, slots), 1)
    places = jnp.zeros((1, slots), jnp.int32)
    for slot in range(slots):
        places = jnp.where(lane == slot, edge_place[slot], places)
    row = lax.broadcasted_iota(jnp.int32, (rows, slots), 0)
    inner_sum = jnp.zeros((rows, inner.shape[2]), F32)
    shared_sum = jnp.zeros((rows, shared.shape[2]), F32)
    for copy in edges:
        copy.wait()
    for k in range(keep):
        pick = jnp.where(row == places + k * capacity, 1.0, 0.0).astype(BF16)
        inner_sum = inner_sum + jnp.dot(pick, inner[k], preferred_element_type=F32)
        shared_sum = shared_sum + jnp.dot(pick, shared[k], preferred_element_type=F32)
    packed = jnp.concatenate([inner_sum, shared_sum], axis=1).astype(BF16)
    lanes = out_edges.shape[2]
    for peer in range(groups):
        for block in range(packed.shape[1] // lanes):
            here = packed[peer * edge_block : (peer + 1) * edge_block, block * lanes : (block + 1) * lanes]
            out_edges[peer, block * edge_block : (block + 1) * edge_block, :] = here

    def from_origin(origin, carry):
        away = ids[origin]

        def one(slot, rank):
            old = origin * slots + slot
            new = place[old] - first
            mine = jnp.logical_and(jnp.logical_and(new >= 0, new < slots), old != away)
            new_slots[jnp.where(mine, origin * stride + rank, dump)] = new
            recv_rows[jnp.where(mine, new, slots)] = origin * edge_block + rank
            return rank + mine.astype(jnp.int32)

        rank = lax.fori_loop(0, slots, one, 0, unroll=8)
        kept[origin] = rank
        new = place[away] - first
        mine = jnp.logical_and(new >= 0, new < slots)
        new_slots[jnp.where(mine, origin * stride + rank, dump)] = new
        return carry

    lax.fori_loop(0, groups, from_origin, 0)

    def migrated(origin, carry):
        new = place[dest[origin]] - first
        mine = jnp.logical_and(new >= 0, new < slots)
        recv_rows[jnp.where(mine, new, slots)] = origin * edge_block + kept[origin]
        return carry

    lax.fori_loop(0, groups, migrated, 0)
    for write in writes:
        write.wait()


def pack(mig_ids, mig_dest, reorder, edge_inner, edge_shared, states, groups, early, capacity, edge_block):
    slots = states.shape[0]
    stride = slots // groups
    width = edge_inner.shape[2] + edge_shared.shape[2]
    lanes = states.shape[3]
    share = states.shape[1] * states.shape[2] // groups
    chunk = 8
    shape = jax.ShapeDtypeStruct
    peers = groups - 1 if early else 0
    inner = edge_inner.transpose(1, 0, 2)
    shared = edge_shared.transpose(1, 0, 2)
    return pl.pallas_call(
        functools.partial(pack_kernel, groups, slots, early, capacity, edge_block, chunk),
        out_shape=(
            shape((slots + 1,), jnp.int32),
            shape((slots + 1,), jnp.int32),
            shape((slots + 1,), jnp.int32),
            shape((groups, edge_block * width // lanes + (share if share % 16 == 0 else 0), lanes), BF16),
            shape(states.shape[1:], BF16),
            shape((groups,) + states.shape[1:], BF16),
        )
        + (shape((early,) + states.shape[1:], BF16),) * peers,
        in_specs=[HBM] * 6,
        out_specs=(SMEM, SMEM, SMEM, VMEM, HBM, HBM) + (HBM,) * peers,
        scratch_shapes=[
            pltpu.SMEM(mig_ids.shape, jnp.int32),
            pltpu.SMEM(mig_dest.shape, jnp.int32),
            pltpu.SMEM(reorder.shape, jnp.int32),
            pltpu.SMEM(reorder.shape, jnp.int32),
            pltpu.SMEM((slots,), jnp.int32),
            pltpu.SMEM((groups,), jnp.int32),
            pltpu.SMEM((groups,), jnp.int32),
            pltpu.VMEM(states.shape, states.dtype),
            pltpu.VMEM(inner.shape, BF16),
            pltpu.VMEM(shared.shape, BF16),
            pltpu.SemaphoreType.DMA((slots // chunk,)),
            pltpu.SemaphoreType.DMA((1,)),
            pltpu.SemaphoreType.DMA((5,)),
        ],
        compiler_params=pltpu.CompilerParams(vmem_limit_bytes=VMEM_BYTES),
        cost_estimate=CHEAP,
        name="pack",
    )(mig_ids, mig_dest, reorder, inner, shared, states)


def shift_rows(value, by):
    by = by % value.shape[0]
    return pltpu.roll(value, by, 0) if by else value


def mix(edge, fresh, weight, bias, token):
    taps = weight.shape[0]
    summed = fresh * weight[taps - 1 : taps] + bias
    for tap in range(taps - 1):
        back = taps - 1 - tap
        moved = jnp.where(token >= back, shift_rows(fresh, back), shift_rows(edge, -tap))
        summed = summed + moved * weight[tap : tap + 1]
    return summed / (1.0 + jnp.exp(-summed))


def latest(edge, fresh, counts, token, window):
    keep = window - 1
    result = edge
    for length in range(1, window + 1):
        chosen = jnp.where(token + length < keep, shift_rows(edge, -length), shift_rows(fresh, keep - length))
        result = jnp.where(counts == length, chosen, result)
    return result


def token_kernel(
    window,
    heads,
    head_dim,
    state_dim,
    capacity,
    skip_ref,
    recv_ref,
    rows_ref,
    shared_ref,
    edges_ref,
    counts_ref,
    conv_inner_ref,
    inner_bias_ref,
    conv_shared_ref,
    shared_bias_ref,
    step_bias_ref,
    decay_log_ref,
    moved_ref,
    entry_ref,
    readout_ref,
    within_ref,
    decay_ref,
    gate_ref,
    new_inner_ref,
    new_shared_ref,
):
    inner = heads * head_dim
    rows = rows_ref.shape[0]
    wide = lax.broadcasted_iota(jnp.int32, (rows, 1), 0)
    token = lax.rem(wide, window)
    counts = counts_ref[...]
    valid = token < counts

    arrived = edges_ref.shape[0]
    place = jnp.zeros((rows, 1), jnp.int32)
    for slot in range(rows // window):
        place = jnp.where(lax.div(wide, window) == slot, recv_ref[slot], place)
    pick = lax.broadcasted_iota(jnp.int32, (rows, arrived), 1) == place + token * capacity
    pick = jnp.logical_and(pick, token < window - 1)
    edges = jnp.dot(jnp.where(pick, 1.0, 0.0).astype(BF16), edges_ref[...], preferred_element_type=F32)

    gate = rows_ref[:, :inner].astype(F32)
    gate_ref[...] = jnp.where(valid, gate / (1.0 + jnp.exp(-gate)), 0.0)

    value = rows_ref[:, inner:].astype(F32)
    edge = edges[:, :inner]
    keep = window - 1
    slots = rows // window
    row = lax.broadcasted_iota(jnp.int32, (slots, rows), 0)
    lane = lax.broadcasted_iota(jnp.int32, (slots, rows), 1)
    takes = [jnp.where(lane == row * window + k, 1.0, 0.0).astype(BF16) for k in range(keep)]
    newest = latest(edge, value, counts, token, window).astype(BF16)
    for k in range(keep):
        new_inner_ref[k] = jnp.dot(takes[k], newest, preferred_element_type=F32).astype(BF16)
    mixed = mix(edge, value, conv_inner_ref[...], inner_bias_ref[...], token)

    fresh = shared_ref[:, : 2 * state_dim].astype(F32)
    edge = edges[:, inner:]
    newest = latest(edge, fresh, counts, token, window).astype(BF16)
    for k in range(keep):
        new_shared_ref[k] = jnp.dot(takes[k], newest, preferred_element_type=F32).astype(BF16)
    shared = mix(edge, fresh, conv_shared_ref[...], shared_bias_ref[...], token)
    entry = shared[:, :state_dim]
    readout = shared[:, state_dim:]
    entry_ref[...] = entry.astype(BF16)
    readout_t = readout.T.astype(BF16)
    readout_ref[...] = readout_t

    raw = shared_ref[:, 2 * state_dim :]
    all_heads = raw.shape[1]
    from_head = lax.broadcasted_iota(jnp.int32, (all_heads, rows), 0)
    to_lane = lax.broadcasted_iota(jnp.int32, (all_heads, rows), 1)
    pick = jnp.logical_and(from_head == to_lane + lax.axis_index("head") * heads, to_lane < heads)
    raw = jnp.dot(raw, pick.astype(BF16), preferred_element_type=F32) + step_bias_ref[...]
    step = jnp.maximum(raw, 0.0) + jnp.log(1.0 + jnp.exp(-jnp.abs(raw)))
    step = jnp.where(valid, step, 0.0)
    drop = step * -jnp.exp(decay_log_ref[...])
    total = drop
    after = drop
    reach = 1
    while reach < window:
        total = total + jnp.where(token >= reach, shift_rows(total, reach), 0.0)
        after = after + jnp.where(token + reach < window, shift_rows(after, -reach), 0.0)
        reach *= 2
    after = jnp.where(token + 1 < window, shift_rows(after, -1), 0.0)
    total_t = total.T
    decay_ref[...] = jnp.exp(total_t)[: decay_ref.shape[0]]
    carry_t = (step * jnp.exp(after)).T

    slot_a = lax.div(lax.broadcasted_iota(jnp.int32, (rows, rows), 0), window)
    slot_b = lax.div(lax.broadcasted_iota(jnp.int32, (rows, rows), 1), window)
    row_a = lax.broadcasted_iota(jnp.int32, (rows, rows), 0)
    row_b = lax.broadcasted_iota(jnp.int32, (rows, rows), 1)
    causal = jnp.logical_and(slot_a == slot_b, row_a <= row_b)
    overlap = jnp.dot(entry.astype(BF16), readout_t, preferred_element_type=F32)
    overlap = jnp.where(causal, overlap, 0.0)
    for block in range(inner // rows):
        turned = mixed[:, block * rows : (block + 1) * rows].T
        for part in range(rows // head_dim):
            head = block * (rows // head_dim) + part
            mine = turned[part * head_dim : (part + 1) * head_dim]
            here = pl.ds(head * head_dim, head_dim)
            moved_ref[here, :] = (mine * carry_t[head : head + 1]).astype(BF16)
            gap = jnp.minimum(total_t[head : head + 1] - total[:, head : head + 1], 0.0)
            weight = overlap * jnp.exp(gap) * step[:, head : head + 1]
            within_ref[here, :] = skip_ref[head] * mine + jnp.dot(
                mine.astype(BF16), weight.astype(BF16), preferred_element_type=F32
            )


def token_part(
    skip_gain, recv_rows, rows, shared, edges, counts, conv_inner, inner_bias, conv_shared, shared_bias, step_bias, decay_log, window, heads, head_dim, state_dim, capacity
):
    count = rows.shape[0]
    inner = heads * head_dim
    padded = -(-heads // 8) * 8
    shape = jax.ShapeDtypeStruct
    return pl.pallas_call(
        functools.partial(token_kernel, window, heads, head_dim, state_dim, capacity),
        out_shape=(
            shape((inner, count), BF16),
            shape((count, state_dim), BF16),
            shape((state_dim, count), BF16),
            shape((inner, count), F32),
            shape((padded, count), F32),
            shape((count, inner), F32),
            shape((window - 1, count // window, inner), BF16),
            shape((window - 1, count // window, 2 * state_dim), BF16),
        ),
        in_specs=[SMEM] * 2 + [VMEM] * 10,
        out_specs=(VMEM,) * 8,
        compiler_params=pltpu.CompilerParams(vmem_limit_bytes=VMEM_BYTES),
        cost_estimate=CHEAP,
        name="token_rows",
    )(skip_gain, recv_rows, rows, shared, edges, counts, conv_inner, inner_bias, conv_shared, shared_bias, step_bias, decay_log)


def page_jobs(groups, stride, steps, pages, late, states_ref, new_slots, slot_of):
    device = lax.axis_index("req")
    jobs = []
    pages = list(pages)
    for step in steps:
        origin = origin_of(device, step, groups)
        arrived = pages.pop(0) if step else None
        for rank in range(stride - 1):
            at = origin * stride + rank
            jobs.append((arrived.at[rank] if step else states_ref.at[slot_of[at]], new_slots[at]))
    if late is not None:
        jobs += [(late.at[origin], new_slots[origin * stride + stride - 1]) for origin in range(groups)]
    return jobs


def load_pages(jobs, batch, pages_in, read_done):
    return fetch([(source, pages_in.at[n]) for n, (source, _) in enumerate(jobs)], read_done)


def batches(jobs, batch):
    return [range(start, min(start + batch, len(jobs))) for start in range(0, len(jobs), batch)]


def read_pages(window, batch, jobs, loads, pages_in, readout):
    heads, head_dim, state_dim = pages_in.shape[1:]
    count = readout.shape[1]
    lane_slot = lax.div(lax.broadcasted_iota(jnp.int32, (state_dim, count), 1), window)
    total = None
    for group in batches(jobs, batch):
        for n in group:
            loads[n].wait()
        wanted = [jnp.where(lane_slot == jobs[n][1], readout[...], jnp.zeros((), BF16)) for n in group]
        held = jnp.concatenate([pages_in[n].reshape(heads * head_dim, state_dim) for n in group], axis=1)
        read = jnp.dot(held, jnp.concatenate(wanted, axis=0), preferred_element_type=F32)
        total = read if total is None else total + read
    return total


def update_pages(window, batch, jobs, loads, pages_in, pages_out, write_done, out_ref, moved, entry, decay):
    heads, head_dim, state_dim = pages_in.shape[1:]
    count = entry.shape[0]
    row_slot = lax.div(lax.broadcasted_iota(jnp.int32, (count, state_dim), 0), window)
    stores = []
    for group in batches(jobs, batch):
        for n in group if loads else ():
            loads[n].wait()
        entries = [jnp.where(row_slot == jobs[n][1], entry[...], jnp.zeros((), BF16)) for n in group]
        added = jnp.dot(moved[...], jnp.concatenate(entries, axis=1), preferred_element_type=F32)
        for q, n in enumerate(group):
            slot = jobs[n][1]
            lane = slot * window + window - 1
            for head in range(heads):
                here = slice(head * head_dim, (head + 1) * head_dim)
                kept = pages_in[n, head].astype(F32) * decay[head, lane]
                pages_out[n, head] = (kept + added[here, q * state_dim : (q + 1) * state_dim]).astype(BF16)
            stores.append(pltpu.make_async_copy(pages_out.at[n], out_ref.at[slot], write_done.at[0]))
            stores[-1].start()
    return stores


def early_kernel(window, batch, groups, stride, steps, new_slots, slot_of, decay_hbm, moved_hbm, entry_hbm, readout_hbm, states_ref, *refs):
    count = len([step for step in steps if step])
    out_ref, read_ref, moved, entry, readout, decay, pages_in, pages_out, read_done, write_done, small_done = refs[count:]
    pairs = ((decay_hbm, decay), (moved_hbm, moved), (entry_hbm, entry), (readout_hbm, readout))
    small = fetch(pairs, small_done)
    jobs = page_jobs(groups, stride, steps, refs[:count], None, states_ref, new_slots, slot_of)
    loads = load_pages(jobs, batch, pages_in, read_done)
    for copy in small:
        copy.wait()
    read_ref[...] = read_pages(window, batch, jobs, loads, pages_in, readout)
    for store in update_pages(window, batch, jobs, [], pages_in, pages_out, write_done, out_ref, moved, entry, decay):
        store.wait()


def hidden_kernel(
    window,
    batch,
    groups,
    stride,
    shares,
    steps,
    heads,
    head_dim,
    started,
    new_slots,
    decay_hbm,
    readout_hbm,
    within_hbm,
    gate_hbm,
    gain_hbm,
    weight_hbm,
    late,
    *refs,
):
    pages, refs = refs[: len(steps)], refs[len(steps) :]
    read_hbm = refs[0] if started else None
    refs = refs[1 if started else 0 :]
    messages, refs = refs[:shares], refs[shares:]
    readout, decay, within, gate, gain, weight, read, rows_all, pages_in, read_done, small_done = refs
    jobs = page_jobs(groups, stride, steps, pages, late, None, new_slots, None)
    pairs = [(readout_hbm, readout), (decay_hbm, decay), (within_hbm, within), (gate_hbm, gate), (gain_hbm, gain), (weight_hbm, weight)]
    small = fetch(pairs[:1], small_done)
    loads = load_pages(jobs, batch, pages_in, read_done)
    small += fetch(pairs[1:] + ([(read_hbm, read)] if started else []), small_done, 1)
    small[0].wait()
    total = read_pages(window, batch, jobs, loads, pages_in, readout)
    for copy in small[1:]:
        copy.wait()
    read[...] = total + read[...] if started else total
    count, inner = gate.shape
    factor = decay[...]
    blocks = []
    for block in range(inner // count):
        parts = []
        for part in range(count // head_dim):
            head = block * (count // head_dim) + part
            here = pl.ds(head * head_dim, head_dim)
            parts.append(read[here, :] * factor[head : head + 1] + within[here, :])
        blocks.append(jnp.concatenate(parts, axis=0).T)
    gated = jnp.concatenate(blocks, axis=1) * gate[...]
    squares = jnp.sum(gated * gated, axis=1, keepdims=True)
    high = squares.astype(BF16)
    low = (squares - high.astype(F32)).astype(BF16)
    scaled = (gated * gain[...]).astype(BF16)
    width = weight.shape[1]
    rows_all[:, :width] = jnp.dot(scaled, weight[...], preferred_element_type=F32).astype(BF16)
    lane = lax.broadcasted_iota(jnp.int32, (count, rows_all.shape[1] - width), 1)
    rows_all[:, width:] = jnp.where(lane == 0, high, jnp.where(lane == 1, low, jnp.zeros((), BF16)))
    own = count // shares
    for step in range(shares):
        start = peer_of(lax.axis_index("head"), step, shares) * own
        messages[step][...] = rows_all[pl.ds(pl.multiple_of(start, own), own), :]


def update_kernel(window, batch, groups, stride, steps, started, new_slots, decay_hbm, moved_hbm, entry_hbm, late, *refs):
    pages, refs = refs[: len(steps)], refs[len(steps) + (1 if started else 0) :]
    out_ref, moved, entry, decay, pages_in, pages_out, read_done, write_done, small_done = refs
    small = fetch(((decay_hbm, decay), (moved_hbm, moved), (entry_hbm, entry)), small_done)
    jobs = page_jobs(groups, stride, steps, pages, late, None, new_slots, None)
    loads = load_pages(jobs, batch, pages_in, read_done)
    for copy in small:
        copy.wait()
    for store in update_pages(window, batch, jobs, loads, pages_in, pages_out, write_done, out_ref, moved, entry, decay):
        store.wait()


def state_part(new_slots, slot_of, early_pages, steps, late, states, moved, entry, readout, within, decay, gate, gain, out_weight, window, groups, shares):
    slots, heads, head_dim, _ = states.shape
    page = states.shape[1:]
    stride = slots // groups
    count, inner = gate.shape
    width = out_weight.shape[1]
    shape = jax.ShapeDtypeStruct
    new_states = shape(states.shape, BF16)
    batch = 4
    floating = list(range(3, groups - 1, 2))
    rest = [step for step in early_pages if step not in steps]
    others = [early_pages[step] for step in rest]
    params = pltpu.CompilerParams(vmem_limit_bytes=VMEM_BYTES)

    def held(*arrays):
        return [pltpu.VMEM(array.shape, array.dtype) for array in arrays]

    def paging(jobs, copies):
        return [pltpu.VMEM((jobs,) + page, BF16)] * copies + [pltpu.SemaphoreType.DMA((jobs,))]

    done = pltpu.SemaphoreType.DMA
    decay_scalars = pltpu.SMEM(decay.shape, F32)
    read, begun = [], []
    if steps:
        arrived = [early_pages[step] for step in steps if step]
        operands = [new_slots, slot_of, decay, moved, entry, readout, states] + arrived
        out = pl.pallas_call(
            functools.partial(early_kernel, window, batch, groups, stride, steps),
            out_shape=(new_states, shape((inner, count), F32)),
            in_specs=[SMEM] * 2 + [HBM] * (len(operands) - 2),
            out_specs=(HBM, VMEM),
            scratch_shapes=held(moved, entry, readout) + [decay_scalars] + paging(len(steps) * (stride - 1), 2) + [done((1,)), done((4,))],
            compiler_params=params,
            cost_estimate=pl.CostEstimate(flops=12_000_000_000, bytes_accessed=1, transcendentals=0),
            name="early_pages",
        )(*operands)
        begun, read = [out[0]], [out[1]]
    jobs = groups + len(rest) * (stride - 1)
    operands = [new_slots, decay, readout, within, gate, gain, out_weight, late] + others + read
    message = shape((count // shares, width + 128), BF16)
    messages = pl.pallas_call(
        functools.partial(hidden_kernel, window, batch, groups, stride, shares, rest, heads, head_dim, bool(read)),
        out_shape=(message,) * shares,
        in_specs=[SMEM] + [HBM] * (len(operands) - 1),
        out_specs=(VMEM,) * shares,
        scratch_shapes=held(readout, decay, within, gate, gain, out_weight, within)
        + [pltpu.VMEM((count, width + 128), BF16)]
        + paging(jobs, 1)
        + [done((7,))],
        compiler_params=params,
        cost_estimate=CHEAP,
        name="hidden_rows",
    )(*operands)
    operands = [new_slots, decay, moved, entry, late] + others + begun
    out = pl.pallas_call(
        functools.partial(update_kernel, window, batch, groups, stride, rest, bool(begun)),
        out_shape=new_states,
        in_specs=[SMEM] + [HBM] * (len(operands) - 1),
        out_specs=HBM,
        scratch_shapes=held(moved, entry) + [decay_scalars] + paging(jobs, 2) + [done((1,)), done((3,))],
        input_output_aliases={len(operands) - 1: 0} if begun else {},
        compiler_params=params,
        cost_estimate=pl.CostEstimate(flops=1, bytes_accessed=4 * states.size, transcendentals=0),
        name="late_pages",
    )(*operands)
    return out, messages


def finish_kernel(full, tokens_hbm, *refs):
    count = (len(refs) - 3) // 2
    hbm, out_ref, tokens, held, done = refs[:count], refs[count], refs[count + 1], refs[count + 2 : -1], refs[-1]
    copies = fetch([(tokens_hbm, tokens)] + list(zip(hbm, held)), done)
    for copy in copies:
        copy.wait()
    total = held[0][...].astype(F32)
    for message in held[1:]:
        total = total + message[...].astype(F32)
    width = tokens.shape[1]
    squares = total[:, width : width + 1] + total[:, width + 1 : width + 2]
    mixer = total[:, :width] * lax.rsqrt(squares / full + EPS)
    out_ref[...] = (tokens[...].astype(F32) + mixer).astype(BF16)


def finish(tokens, messages, full):
    return pl.pallas_call(
        functools.partial(finish_kernel, full),
        out_shape=jax.ShapeDtypeStruct(tokens.shape, BF16),
        in_specs=[HBM] * (1 + len(messages)),
        out_specs=VMEM,
        scratch_shapes=[pltpu.VMEM(array.shape, BF16) for array in [tokens] + messages]
        + [pltpu.SemaphoreType.DMA((1 + len(messages),))],
        compiler_params=pltpu.CompilerParams(vmem_limit_bytes=VMEM_BYTES),
        cost_estimate=CHEAP,
        name="finish",
    )(tokens, *messages)


def local(
    tokens,
    pre_gain,
    inner_weight,
    shared_weight,
    conv_inner,
    conv_inner_bias,
    conv_shared,
    conv_shared_bias,
    step_bias,
    decay_log,
    skip_gain,
    gate_gain,
    out_weight,
    states,
    edge_inner,
    edge_shared,
    counts,
    mig_ids,
    mig_dest,
    reorder,
):
    slots, heads, head_dim, state_dim = states.shape
    inner = heads * head_dim
    groups = lax.axis_size("req")
    shares = lax.axis_size("head")
    request_index = lax.axis_index("req")
    head_index = lax.axis_index("head")
    own_rows = tokens.shape[0]
    window = own_rows * shares // slots
    width = tokens.shape[1]
    stride = slots // groups
    keep = edge_inner.shape[1]
    early = stride - 1
    capacity = stride + 1
    edge_block = -(-keep * capacity // 16) * 16
    exchange = functools.partial(lax.all_to_all, axis_name="req", split_axis=0, concat_axis=0, tiled=True)

    packed = pack(mig_ids, mig_dest, reorder, edge_inner, edge_shared, states, groups, early, capacity, edge_block)
    slot_of, recv_rows, new_slots, send_edges, page, send_late = packed[:6]
    sent = dict(enumerate(packed[6:], 1))
    behind = [1, groups - 2, groups - 1] if len(sent) > 2 else []
    early_pages = {step: permute(sent[step], "req", step) for step in sent if step not in behind}
    first = list(range(2, groups, 2))[:2] if early_pages else []
    floating = list(range(3, groups - 1, 2))
    rest = [step for step in range(2, groups) if step not in first] if early_pages else []
    edge_rows = edge_block * (inner + 2 * state_dim) // state_dim
    if send_edges.shape[1] == edge_rows:
        send_edges = jnp.concatenate([send_edges, page.reshape(groups, inner // groups, state_dim)], axis=1)
    pieces = exchange(send_edges)
    edges = pieces[:, :edge_rows].reshape(groups, -1, edge_block, state_dim).transpose(0, 2, 1, 3)
    edges = edges.reshape(groups * edge_block, -1)
    rows_in = tokens.astype(F32)
    normed = (rows_in * lax.rsqrt(jnp.mean(rows_in * rows_in, axis=-1, keepdims=True) + EPS) * pre_gain).astype(BF16)
    comes_from = jnp.argmax(mig_dest[None, :] == mig_ids[:, None], axis=1)
    pieces = pieces[comes_from, edge_rows:]
    arrived = exchange(pieces)
    for step in behind:
        waiting, _ = lax.optimization_barrier((sent[step], pieces if step == groups - 2 else arrived))
        early_pages[step] = permute(waiting, "req", step)
    arrived = arrived.reshape(states.shape[1:])
    all_rows = lax.all_gather(normed, "head", axis=0, tiled=True)
    all_rows, inner_weight, _ = lax.optimization_barrier((all_rows, inner_weight, pieces))
    leaving = lax.dynamic_index_in_dim(mig_ids, request_index, 0, keepdims=False)
    target = jnp.argmax(reorder == leaving) // slots
    inner_flat = inner_weight.reshape(width, 2 * inner)
    inner_rows = jnp.dot(all_rows, inner_flat, preferred_element_type=F32).astype(BF16)
    shared_rows = jnp.dot(all_rows, shared_weight, preferred_element_type=F32).astype(BF16)

    lanes = slots * window

    def in_lanes(vector):
        return jnp.pad(vector, (0, lanes - heads)).reshape(1, lanes)

    moved, entry, readout, within, decay, gate, new_inner, new_shared = token_part(
        skip_gain,
        recv_rows,
        inner_rows,
        shared_rows,
        edges,
        jnp.repeat(counts, window).reshape(lanes, 1),
        conv_inner,
        conv_inner_bias.reshape(1, -1),
        conv_shared,
        conv_shared_bias.reshape(1, -1),
        in_lanes(step_bias),
        in_lanes(decay_log),
        window,
        heads,
        head_dim,
        state_dim,
        capacity,
    )
    late = exchange(lax.dynamic_update_index_in_dim(send_late, arrived, target, 0))
    edge_inner_out = new_inner.transpose(1, 0, 2)
    edge_shared_out = new_shared.transpose(1, 0, 2)

    states_out, messages = state_part(
        new_slots,
        slot_of,
        early_pages,
        list(range(groups)) if sent else [],
        late,
        states,
        moved,
        entry,
        readout,
        within,
        decay,
        gate,
        gate_gain.reshape(1, -1),
        out_weight,
        window,
        groups,
        shares,
    )
    messages = [permute(messages[step], "head", step) for step in range(shares - 1, 0, -1)] + [messages[0]]
    hidden_out = finish(tokens, messages, inner * shares)
    return (hidden_out, states_out, edge_inner_out, edge_shared_out)


def solution(mesh):
    placed = (
        P(("req", "head"), None),
        P(),
        P(None, None, "head"),
        P(),
        P(None, "head"),
        P("head"),
        P(),
        P(),
        P("head"),
        P("head"),
        P("head"),
        P("head"),
        P("head", None),
        P("req", "head", None, None),
        P("req", None, "head"),
        P("req", None, None),
        P("req"),
        P(),
        P(),
        P(),
    )
    return jax.shard_map(
        local,
        mesh=mesh,
        in_specs=placed,
        out_specs=(
            P(("req", "head"), None),
            P("req", "head", None, None),
            P("req", None, "head"),
            P("req", None, None),
        ),
        check_vma=False,
    )
```

```python
import functools

import jax
import jax.numpy as jnp
from jax import lax
from jax.experimental import pallas as pl
from jax.experimental.pallas import tpu as pltpu
from jax.sharding import PartitionSpec as P

EPS = 1e-05
F32 = jnp.float32
BF16 = jnp.bfloat16
VMEM_BYTES = 63 * 1024 * 1024
CHEAP = pl.CostEstimate(flops=1, bytes_accessed=1, transcendentals=0)
HBM = pl.BlockSpec(memory_space=pltpu.HBM)
SMEM = pl.BlockSpec(memory_space=pltpu.SMEM)
VMEM = pl.BlockSpec(memory_space=pltpu.VMEM)


def peer_of(index, step, size):
    if size & (size - 1) == 0:
        return index ^ step
    return lax.rem(index + step, size)


def origin_of(index, step, size):
    if size & (size - 1) == 0:
        return index ^ step
    return lax.rem(index - step + size, size)


def permute(value, axis, step):
    size = lax.axis_size(axis)
    pairs = [(i, i ^ step if size & (size - 1) == 0 else (i + step) % size) for i in range(size)]
    return lax.ppermute(value, axis, pairs)


def invert(order, place):
    def one(slot, carry):
        place[order[slot]] = slot
        return carry

    lax.fori_loop(0, order.shape[0], one, 0, unroll=16)


def fetch(pairs, done, first=0):
    copies = [pltpu.make_async_copy(source, target, done.at[first + n]) for n, (source, target) in enumerate(pairs)]
    for copy in copies:
        copy.start()
    return copies


def pack_kernel(
    groups,
    slots,
    early,
    capacity,
    edge_block,
    chunk,
    ids_hbm,
    dest_hbm,
    reorder_hbm,
    inner_hbm,
    shared_hbm,
    states_ref,
    slot_of,
    recv_rows,
    new_slots,
    out_edges,
    leaving,
    out_late,
    *refs,
):
    out_early = refs[: groups - 1] if early else []
    ids, dest, reorder, place, edge_place, seen, kept, staged, inner, shared, read_done, write_done, small_done = refs[len(out_early) :]
    stride = slots // groups
    device = lax.axis_index("req")
    first = device * slots
    small = fetch(((ids_hbm, ids), (dest_hbm, dest), (reorder_hbm, reorder)), small_done)
    parts = [pl.ds(part * chunk, chunk) for part in range(slots // chunk)]
    reads = fetch([(states_ref.at[part], staged.at[part]) for part in parts], read_done)
    edges = fetch(((inner_hbm, inner), (shared_hbm, shared)), small_done, 3)
    for copy in small:
        copy.wait()
    invert(reorder, place)
    for group in range(groups):
        seen[group] = 0
    moving = ids[device] - first
    dump = groups * stride

    def to_peer(slot, carry):
        peer = lax.div(place[first + slot], slots)
        rank = seen[peer]
        stays = slot != moving
        slot_of[jnp.where(stays, peer * stride + rank, dump)] = slot
        edge_place[slot] = peer * edge_block + rank
        seen[peer] = rank + stays.astype(jnp.int32)
        return carry

    lax.fori_loop(0, slots, to_peer, 0, unroll=4)
    peer = lax.div(place[dest[device]], slots)
    edge_place[moving] = peer * edge_block + seen[peer]
    peer = lax.div(place[first + moving], slots)
    slot_of[peer * stride + seen[peer]] = moving

    jobs = [(moving, leaving)]
    for step in range(1, groups):
        peer = peer_of(device, step, groups)
        jobs += [(slot_of[peer * stride + rank], out_early[step - 1].at[rank]) for rank in range(early)]
    jobs += [(slot_of[peer * stride + stride - 1], out_late.at[peer]) for peer in range(groups)]
    writes = [pltpu.make_async_copy(staged.at[slot], target, write_done.at[0]) for slot, target in jobs]
    for part, read in enumerate(reads):
        read.wait()
        for (slot, _), write in zip(jobs, writes):
            pl.when(lax.div(slot, chunk) == part)(write.start)

    pieces = staged[moving].reshape(-1, staged.shape[3])
    edge_rows = edge_block * (inner.shape[2] + shared.shape[2]) // staged.shape[3]
    share = pieces.shape[0] // groups
    if out_edges.shape[1] > edge_rows:
        for peer in range(groups):
            out_edges[peer, edge_rows:, :] = pieces[peer * share : (peer + 1) * share]
    keep = inner.shape[0]
    rows = groups * edge_block
    lane = lax.broadcasted_iota(jnp.int32, (1, slots), 1)
    places = jnp.zeros((1, slots), jnp.int32)
    for slot in range(slots):
        places = jnp.where(lane == slot, edge_place[slot], places)
    row = lax.broadcasted_iota(jnp.int32, (rows, slots), 0)
    inner_sum = jnp.zeros((rows, inner.shape[2]), F32)
    shared_sum = jnp.zeros((rows, shared.shape[2]), F32)
    for copy in edges:
        copy.wait()
    for k in range(keep):
        pick = jnp.where(row == places + k * capacity, 1.0, 0.0).astype(BF16)
        inner_sum = inner_sum + jnp.dot(pick, inner[k], preferred_element_type=F32)
        shared_sum = shared_sum + jnp.dot(pick, shared[k], preferred_element_type=F32)
    packed = jnp.concatenate([inner_sum, shared_sum], axis=1).astype(BF16)
    lanes = out_edges.shape[2]
    for peer in range(groups):
        for block in range(packed.shape[1] // lanes):
            here = packed[peer * edge_block : (peer + 1) * edge_block, block * lanes : (block + 1) * lanes]
            out_edges[peer, block * edge_block : (block + 1) * edge_block, :] = here

    def from_origin(origin, carry):
        away = ids[origin]

        def one(slot, rank):
            old = origin * slots + slot
            new = place[old] - first
            mine = jnp.logical_and(jnp.logical_and(new >= 0, new < slots), old != away)
            new_slots[jnp.where(mine, origin * stride + rank, dump)] = new
            recv_rows[jnp.where(mine, new, slots)] = origin * edge_block + rank
            return rank + mine.astype(jnp.int32)

        rank = lax.fori_loop(0, slots, one, 0, unroll=8)
        kept[origin] = rank
        new = place[away] - first
        mine = jnp.logical_and(new >= 0, new < slots)
        new_slots[jnp.where(mine, origin * stride + rank, dump)] = new
        return carry

    lax.fori_loop(0, groups, from_origin, 0)

    def migrated(origin, carry):
        new = place[dest[origin]] - first
        mine = jnp.logical_and(new >= 0, new < slots)
        recv_rows[jnp.where(mine, new, slots)] = origin * edge_block + kept[origin]
        return carry

    lax.fori_loop(0, groups, migrated, 0)
    for write in writes:
        write.wait()


def pack(mig_ids, mig_dest, reorder, edge_inner, edge_shared, states, groups, early, capacity, edge_block):
    slots = states.shape[0]
    stride = slots // groups
    width = edge_inner.shape[2] + edge_shared.shape[2]
    lanes = states.shape[3]
    share = states.shape[1] * states.shape[2] // groups
    chunk = 8
    shape = jax.ShapeDtypeStruct
    peers = groups - 1 if early else 0
    inner = edge_inner.transpose(1, 0, 2)
    shared = edge_shared.transpose(1, 0, 2)
    return pl.pallas_call(
        functools.partial(pack_kernel, groups, slots, early, capacity, edge_block, chunk),
        out_shape=(
            shape((slots + 1,), jnp.int32),
            shape((slots + 1,), jnp.int32),
            shape((slots + 1,), jnp.int32),
            shape((groups, edge_block * width // lanes + (share if share % 16 == 0 else 0), lanes), BF16),
            shape(states.shape[1:], BF16),
            shape((groups,) + states.shape[1:], BF16),
        )
        + (shape((early,) + states.shape[1:], BF16),) * peers,
        in_specs=[HBM] * 6,
        out_specs=(SMEM, SMEM, SMEM, VMEM, HBM, HBM) + (HBM,) * peers,
        scratch_shapes=[
            pltpu.SMEM(mig_ids.shape, jnp.int32),
            pltpu.SMEM(mig_dest.shape, jnp.int32),
            pltpu.SMEM(reorder.shape, jnp.int32),
            pltpu.SMEM(reorder.shape, jnp.int32),
            pltpu.SMEM((slots,), jnp.int32),
            pltpu.SMEM((groups,), jnp.int32),
            pltpu.SMEM((groups,), jnp.int32),
            pltpu.VMEM(states.shape, states.dtype),
            pltpu.VMEM(inner.shape, BF16),
            pltpu.VMEM(shared.shape, BF16),
            pltpu.SemaphoreType.DMA((slots // chunk,)),
            pltpu.SemaphoreType.DMA((1,)),
            pltpu.SemaphoreType.DMA((5,)),
        ],
        compiler_params=pltpu.CompilerParams(vmem_limit_bytes=VMEM_BYTES),
        cost_estimate=CHEAP,
        name="pack",
    )(mig_ids, mig_dest, reorder, inner, shared, states)


def shift_rows(value, by):
    by = by % value.shape[0]
    return pltpu.roll(value, by, 0) if by else value


def mix(edge, fresh, weight, bias, token):
    taps = weight.shape[0]
    summed = fresh * weight[taps - 1 : taps] + bias
    for tap in range(taps - 1):
        back = taps - 1 - tap
        moved = jnp.where(token >= back, shift_rows(fresh, back), shift_rows(edge, -tap))
        summed = summed + moved * weight[tap : tap + 1]
    return summed / (1.0 + jnp.exp(-summed))


def latest(edge, fresh, counts, token, window):
    keep = window - 1
    result = edge
    for length in range(1, window + 1):
        chosen = jnp.where(token + length < keep, shift_rows(edge, -length), shift_rows(fresh, keep - length))
        result = jnp.where(counts == length, chosen, result)
    return result


def token_kernel(
    window,
    heads,
    head_dim,
    state_dim,
    capacity,
    skip_ref,
    recv_ref,
    rows_ref,
    shared_ref,
    edges_ref,
    counts_ref,
    conv_inner_ref,
    inner_bias_ref,
    conv_shared_ref,
    shared_bias_ref,
    step_bias_ref,
    decay_log_ref,
    moved_ref,
    entry_ref,
    readout_ref,
    within_ref,
    decay_ref,
    gate_ref,
    new_inner_ref,
    new_shared_ref,
):
    inner = heads * head_dim
    rows = rows_ref.shape[0]
    wide = lax.broadcasted_iota(jnp.int32, (rows, 1), 0)
    token = lax.rem(wide, window)
    counts = counts_ref[...]
    valid = token < counts

    arrived = edges_ref.shape[0]
    place = jnp.zeros((rows, 1), jnp.int32)
    for slot in range(rows // window):
        place = jnp.where(lax.div(wide, window) == slot, recv_ref[slot], place)
    pick = lax.broadcasted_iota(jnp.int32, (rows, arrived), 1) == place + token * capacity
    pick = jnp.logical_and(pick, token < window - 1)
    edges = jnp.dot(jnp.where(pick, 1.0, 0.0).astype(BF16), edges_ref[...], preferred_element_type=F32)

    gate = rows_ref[:, :inner].astype(F32)
    gate_ref[...] = jnp.where(valid, gate / (1.0 + jnp.exp(-gate)), 0.0)

    value = rows_ref[:, inner:].astype(F32)
    edge = edges[:, :inner]
    keep = window - 1
    slots = rows // window
    row = lax.broadcasted_iota(jnp.int32, (slots, rows), 0)
    lane = lax.broadcasted_iota(jnp.int32, (slots, rows), 1)
    takes = [jnp.where(lane == row * window + k, 1.0, 0.0).astype(BF16) for k in range(keep)]
    newest = latest(edge, value, counts, token, window).astype(BF16)
    for k in range(keep):
        new_inner_ref[k] = jnp.dot(takes[k], newest, preferred_element_type=F32).astype(BF16)
    mixed = mix(edge, value, conv_inner_ref[...], inner_bias_ref[...], token)

    fresh = shared_ref[:, : 2 * state_dim].astype(F32)
    edge = edges[:, inner:]
    newest = latest(edge, fresh, counts, token, window).astype(BF16)
    for k in range(keep):
        new_shared_ref[k] = jnp.dot(takes[k], newest, preferred_element_type=F32).astype(BF16)
    shared = mix(edge, fresh, conv_shared_ref[...], shared_bias_ref[...], token)
    entry = shared[:, :state_dim]
    readout = shared[:, state_dim:]
    entry_ref[...] = entry.astype(BF16)
    readout_t = readout.T.astype(BF16)
    readout_ref[...] = readout_t

    raw = shared_ref[:, 2 * state_dim :]
    all_heads = raw.shape[1]
    from_head = lax.broadcasted_iota(jnp.int32, (all_heads, rows), 0)
    to_lane = lax.broadcasted_iota(jnp.int32, (all_heads, rows), 1)
    pick = jnp.logical_and(from_head == to_lane + lax.axis_index("head") * heads, to_lane < heads)
    raw = jnp.dot(raw, pick.astype(BF16), preferred_element_type=F32) + step_bias_ref[...]
    step = jnp.maximum(raw, 0.0) + jnp.log(1.0 + jnp.exp(-jnp.abs(raw)))
    step = jnp.where(valid, step, 0.0)
    drop = step * -jnp.exp(decay_log_ref[...])
    total = drop
    after = drop
    reach = 1
    while reach < window:
        total = total + jnp.where(token >= reach, shift_rows(total, reach), 0.0)
        after = after + jnp.where(token + reach < window, shift_rows(after, -reach), 0.0)
        reach *= 2
    after = jnp.where(token + 1 < window, shift_rows(after, -1), 0.0)
    total_t = total.T
    decay_ref[...] = jnp.exp(total_t)[: decay_ref.shape[0]]
    carry_t = (step * jnp.exp(after)).T

    slot_a = lax.div(lax.broadcasted_iota(jnp.int32, (rows, rows), 0), window)
    slot_b = lax.div(lax.broadcasted_iota(jnp.int32, (rows, rows), 1), window)
    row_a = lax.broadcasted_iota(jnp.int32, (rows, rows), 0)
    row_b = lax.broadcasted_iota(jnp.int32, (rows, rows), 1)
    causal = jnp.logical_and(slot_a == slot_b, row_a <= row_b)
    overlap = jnp.dot(entry.astype(BF16), readout_t, preferred_element_type=F32)
    overlap = jnp.where(causal, overlap, 0.0)
    for block in range(inner // rows):
        turned = mixed[:, block * rows : (block + 1) * rows].T
        for part in range(rows // head_dim):
            head = block * (rows // head_dim) + part
            mine = turned[part * head_dim : (part + 1) * head_dim]
            here = pl.ds(head * head_dim, head_dim)
            moved_ref[here, :] = (mine * carry_t[head : head + 1]).astype(BF16)
            gap = jnp.minimum(total_t[head : head + 1] - total[:, head : head + 1], 0.0)
            weight = overlap * jnp.exp(gap) * step[:, head : head + 1]
            within_ref[here, :] = skip_ref[head] * mine + jnp.dot(
                mine.astype(BF16), weight.astype(BF16), preferred_element_type=F32
            )


def token_part(
    skip_gain, recv_rows, rows, shared, edges, counts, conv_inner, inner_bias, conv_shared, shared_bias, step_bias, decay_log, window, heads, head_dim, state_dim, capacity
):
    count = rows.shape[0]
    inner = heads * head_dim
    padded = -(-heads // 8) * 8
    shape = jax.ShapeDtypeStruct
    return pl.pallas_call(
        functools.partial(token_kernel, window, heads, head_dim, state_dim, capacity),
        out_shape=(
            shape((inner, count), BF16),
            shape((count, state_dim), BF16),
            shape((state_dim, count), BF16),
            shape((inner, count), F32),
            shape((padded, count), F32),
            shape((count, inner), F32),
            shape((window - 1, count // window, inner), BF16),
            shape((window - 1, count // window, 2 * state_dim), BF16),
        ),
        in_specs=[SMEM] * 2 + [VMEM] * 10,
        out_specs=(VMEM,) * 8,
        compiler_params=pltpu.CompilerParams(vmem_limit_bytes=VMEM_BYTES),
        cost_estimate=CHEAP,
        name="token_rows",
    )(skip_gain, recv_rows, rows, shared, edges, counts, conv_inner, inner_bias, conv_shared, shared_bias, step_bias, decay_log)


def page_jobs(groups, stride, steps, pages, late, states_ref, new_slots, slot_of):
    device = lax.axis_index("req")
    jobs = []
    pages = list(pages)
    for step in steps:
        origin = origin_of(device, step, groups)
        arrived = pages.pop(0) if step else None
        for rank in range(stride - 1):
            at = origin * stride + rank
            jobs.append((arrived.at[rank] if step else states_ref.at[slot_of[at]], new_slots[at]))
    if late is not None:
        jobs += [(late.at[origin], new_slots[origin * stride + stride - 1]) for origin in range(groups)]
    return jobs


def load_pages(jobs, batch, pages_in, read_done):
    return fetch([(source, pages_in.at[n]) for n, (source, _) in enumerate(jobs)], read_done)


def batches(jobs, batch):
    return [range(start, min(start + batch, len(jobs))) for start in range(0, len(jobs), batch)]


def read_pages(window, batch, jobs, loads, pages_in, readout):
    heads, head_dim, state_dim = pages_in.shape[1:]
    count = readout.shape[1]
    lane_slot = lax.div(lax.broadcasted_iota(jnp.int32, (state_dim, count), 1), window)
    total = None
    for group in batches(jobs, batch):
        for n in group:
            loads[n].wait()
        wanted = [jnp.where(lane_slot == jobs[n][1], readout[...], jnp.zeros((), BF16)) for n in group]
        held = jnp.concatenate([pages_in[n].reshape(heads * head_dim, state_dim) for n in group], axis=1)
        read = jnp.dot(held, jnp.concatenate(wanted, axis=0), preferred_element_type=F32)
        total = read if total is None else total + read
    return total


def update_pages(window, batch, jobs, loads, pages_in, pages_out, write_done, out_ref, moved, entry, decay):
    heads, head_dim, state_dim = pages_in.shape[1:]
    count = entry.shape[0]
    row_slot = lax.div(lax.broadcasted_iota(jnp.int32, (count, state_dim), 0), window)
    stores = []
    for group in batches(jobs, batch):
        for n in group if loads else ():
            loads[n].wait()
        entries = [jnp.where(row_slot == jobs[n][1], entry[...], jnp.zeros((), BF16)) for n in group]
        added = jnp.dot(moved[...], jnp.concatenate(entries, axis=1), preferred_element_type=F32)
        for q, n in enumerate(group):
            slot = jobs[n][1]
            lane = slot * window + window - 1
            for head in range(heads):
                here = slice(head * head_dim, (head + 1) * head_dim)
                kept = pages_in[n, head].astype(F32) * decay[head, lane]
                pages_out[n, head] = (kept + added[here, q * state_dim : (q + 1) * state_dim]).astype(BF16)
            stores.append(pltpu.make_async_copy(pages_out.at[n], out_ref.at[slot], write_done.at[0]))
            stores[-1].start()
    return stores


def early_kernel(window, batch, groups, stride, steps, new_slots, slot_of, decay_hbm, moved_hbm, entry_hbm, readout_hbm, states_ref, *refs):
    count = len([step for step in steps if step])
    out_ref, read_ref, moved, entry, readout, decay, pages_in, pages_out, read_done, write_done, small_done = refs[count:]
    pairs = ((decay_hbm, decay), (moved_hbm, moved), (entry_hbm, entry), (readout_hbm, readout))
    small = fetch(pairs, small_done)
    jobs = page_jobs(groups, stride, steps, refs[:count], None, states_ref, new_slots, slot_of)
    loads = load_pages(jobs, batch, pages_in, read_done)
    for copy in small:
        copy.wait()
    read_ref[...] = read_pages(window, batch, jobs, loads, pages_in, readout)
    for store in update_pages(window, batch, jobs, [], pages_in, pages_out, write_done, out_ref, moved, entry, decay):
        store.wait()


def hidden_kernel(
    window,
    batch,
    groups,
    stride,
    shares,
    steps,
    heads,
    head_dim,
    started,
    new_slots,
    decay_hbm,
    readout_hbm,
    within_hbm,
    gate_hbm,
    gain_hbm,
    weight_hbm,
    late,
    *refs,
):
    pages, refs = refs[: len(steps)], refs[len(steps) :]
    read_hbm = refs[0] if started else None
    refs = refs[1 if started else 0 :]
    messages, refs = refs[:shares], refs[shares:]
    readout, decay, within, gate, gain, weight, read, rows_all, pages_in, read_done, small_done = refs
    jobs = page_jobs(groups, stride, steps, pages, late, None, new_slots, None)
    pairs = [(readout_hbm, readout), (decay_hbm, decay), (within_hbm, within), (gate_hbm, gate), (gain_hbm, gain), (weight_hbm, weight)]
    small = fetch(pairs[:1], small_done)
    loads = load_pages(jobs, batch, pages_in, read_done)
    small += fetch(pairs[1:] + ([(read_hbm, read)] if started else []), small_done, 1)
    small[0].wait()
    total = read_pages(window, batch, jobs, loads, pages_in, readout)
    for copy in small[1:]:
        copy.wait()
    read[...] = total + read[...] if started else total
    count, inner = gate.shape
    factor = decay[...]
    blocks = []
    for block in range(inner // count):
        parts = []
        for part in range(count // head_dim):
            head = block * (count // head_dim) + part
            here = pl.ds(head * head_dim, head_dim)
            parts.append(read[here, :] * factor[head : head + 1] + within[here, :])
        blocks.append(jnp.concatenate(parts, axis=0).T)
    gated = jnp.concatenate(blocks, axis=1) * gate[...]
    squares = jnp.sum(gated * gated, axis=1, keepdims=True)
    high = squares.astype(BF16)
    low = (squares - high.astype(F32)).astype(BF16)
    scaled = (gated * gain[...]).astype(BF16)
    width = weight.shape[1]
    rows_all[:, :width] = jnp.dot(scaled, weight[...], preferred_element_type=F32).astype(BF16)
    lane = lax.broadcasted_iota(jnp.int32, (count, rows_all.shape[1] - width), 1)
    rows_all[:, width:] = jnp.where(lane == 0, high, jnp.where(lane == 1, low, jnp.zeros((), BF16)))
    own = count // shares
    for step in range(shares):
        start = peer_of(lax.axis_index("head"), step, shares) * own
        messages[step][...] = rows_all[pl.ds(pl.multiple_of(start, own), own), :]


def update_kernel(window, batch, groups, stride, steps, started, new_slots, decay_hbm, moved_hbm, entry_hbm, late, *refs):
    pages, refs = refs[: len(steps)], refs[len(steps) + (1 if started else 0) :]
    out_ref, moved, entry, decay, pages_in, pages_out, read_done, write_done, small_done = refs
    small = fetch(((decay_hbm, decay), (moved_hbm, moved), (entry_hbm, entry)), small_done)
    jobs = page_jobs(groups, stride, steps, pages, late, None, new_slots, None)
    loads = load_pages(jobs, batch, pages_in, read_done)
    for copy in small:
        copy.wait()
    for store in update_pages(window, batch, jobs, loads, pages_in, pages_out, write_done, out_ref, moved, entry, decay):
        store.wait()


def state_part(new_slots, slot_of, early_pages, steps, late, states, moved, entry, readout, within, decay, gate, gain, out_weight, window, groups, shares):
    slots, heads, head_dim, _ = states.shape
    page = states.shape[1:]
    stride = slots // groups
    count, inner = gate.shape
    width = out_weight.shape[1]
    shape = jax.ShapeDtypeStruct
    new_states = shape(states.shape, BF16)
    batch = 4
    floating = list(range(3, groups - 1, 2))
    rest = [step for step in early_pages if step not in steps]
    others = [early_pages[step] for step in rest]
    params = pltpu.CompilerParams(vmem_limit_bytes=VMEM_BYTES)

    def held(*arrays):
        return [pltpu.VMEM(array.shape, array.dtype) for array in arrays]

    def paging(jobs, copies):
        return [pltpu.VMEM((jobs,) + page, BF16)] * copies + [pltpu.SemaphoreType.DMA((jobs,))]

    done = pltpu.SemaphoreType.DMA
    decay_scalars = pltpu.SMEM(decay.shape, F32)
    read, begun = [], []
    if steps:
        arrived = [early_pages[step] for step in steps if step]
        operands = [new_slots, slot_of, decay, moved, entry, readout, states] + arrived
        out = pl.pallas_call(
            functools.partial(early_kernel, window, batch, groups, stride, steps),
            out_shape=(new_states, shape((inner, count), F32)),
            in_specs=[SMEM] * 2 + [HBM] * (len(operands) - 2),
            out_specs=(HBM, VMEM),
            scratch_shapes=held(moved, entry, readout) + [decay_scalars] + paging(len(steps) * (stride - 1), 2) + [done((1,)), done((4,))],
            compiler_params=params,
            cost_estimate=pl.CostEstimate(flops=12_000_000_000, bytes_accessed=1, transcendentals=0),
            name="early_pages",
        )(*operands)
        begun, read = [out[0]], [out[1]]
    jobs = groups + len(rest) * (stride - 1)
    operands = [new_slots, decay, readout, within, gate, gain, out_weight, late] + others + read
    message = shape((count // shares, width + 128), BF16)
    messages = pl.pallas_call(
        functools.partial(hidden_kernel, window, batch, groups, stride, shares, rest, heads, head_dim, bool(read)),
        out_shape=(message,) * shares,
        in_specs=[SMEM] + [HBM] * (len(operands) - 1),
        out_specs=(VMEM,) * shares,
        scratch_shapes=held(readout, decay, within, gate, gain, out_weight, within)
        + [pltpu.VMEM((count, width + 128), BF16)]
        + paging(jobs, 1)
        + [done((7,))],
        compiler_params=params,
        cost_estimate=CHEAP,
        name="hidden_rows",
    )(*operands)
    operands = [new_slots, decay, moved, entry, late] + others + begun
    out = pl.pallas_call(
        functools.partial(update_kernel, window, batch, groups, stride, rest, bool(begun)),
        out_shape=new_states,
        in_specs=[SMEM] + [HBM] * (len(operands) - 1),
        out_specs=HBM,
        scratch_shapes=held(moved, entry) + [decay_scalars] + paging(jobs, 2) + [done((1,)), done((3,))],
        input_output_aliases={len(operands) - 1: 0} if begun else {},
        compiler_params=params,
        cost_estimate=pl.CostEstimate(flops=1, bytes_accessed=4 * states.size, transcendentals=0),
        name="late_pages",
    )(*operands)
    return out, messages


def finish_kernel(full, tokens_hbm, *refs):
    count = (len(refs) - 3) // 2
    hbm, out_ref, tokens, held, done = refs[:count], refs[count], refs[count + 1], refs[count + 2 : -1], refs[-1]
    copies = fetch([(tokens_hbm, tokens)] + list(zip(hbm, held)), done)
    for copy in copies:
        copy.wait()
    total = held[0][...].astype(F32)
    for message in held[1:]:
        total = total + message[...].astype(F32)
    width = tokens.shape[1]
    squares = total[:, width : width + 1] + total[:, width + 1 : width + 2]
    mixer = total[:, :width] * lax.rsqrt(squares / full + EPS)
    out_ref[...] = (tokens[...].astype(F32) + mixer).astype(BF16)


def finish(tokens, messages, full):
    return pl.pallas_call(
        functools.partial(finish_kernel, full),
        out_shape=jax.ShapeDtypeStruct(tokens.shape, BF16),
        in_specs=[HBM] * (1 + len(messages)),
        out_specs=VMEM,
        scratch_shapes=[pltpu.VMEM(array.shape, BF16) for array in [tokens] + messages]
        + [pltpu.SemaphoreType.DMA((1 + len(messages),))],
        compiler_params=pltpu.CompilerParams(vmem_limit_bytes=VMEM_BYTES),
        cost_estimate=CHEAP,
        name="finish",
    )(tokens, *messages)


def local(
    tokens,
    pre_gain,
    inner_weight,
    shared_weight,
    conv_inner,
    conv_inner_bias,
    conv_shared,
    conv_shared_bias,
    step_bias,
    decay_log,
    skip_gain,
    gate_gain,
    out_weight,
    states,
    edge_inner,
    edge_shared,
    counts,
    mig_ids,
    mig_dest,
    reorder,
):
    slots, heads, head_dim, state_dim = states.shape
    inner = heads * head_dim
    groups = lax.axis_size("req")
    shares = lax.axis_size("head")
    request_index = lax.axis_index("req")
    head_index = lax.axis_index("head")
    own_rows = tokens.shape[0]
    window = own_rows * shares // slots
    width = tokens.shape[1]
    stride = slots // groups
    keep = edge_inner.shape[1]
    early = stride - 1
    capacity = stride + 1
    edge_block = -(-keep * capacity // 16) * 16
    exchange = functools.partial(lax.all_to_all, axis_name="req", split_axis=0, concat_axis=0, tiled=True)

    packed = pack(mig_ids, mig_dest, reorder, edge_inner, edge_shared, states, groups, early, capacity, edge_block)
    slot_of, recv_rows, new_slots, send_edges, page, send_late = packed[:6]
    sent = dict(enumerate(packed[6:], 1))
    behind = [1, groups - 2, groups - 1] if len(sent) > 2 else []
    early_pages = {step: permute(sent[step], "req", step) for step in sent if step not in behind}
    first = list(range(2, groups, 2))[:2] if early_pages else []
    floating = list(range(3, groups - 1, 2))
    rest = [step for step in range(2, groups) if step not in first] if early_pages else []
    edge_rows = edge_block * (inner + 2 * state_dim) // state_dim
    if send_edges.shape[1] == edge_rows:
        send_edges = jnp.concatenate([send_edges, page.reshape(groups, inner // groups, state_dim)], axis=1)
    pieces = exchange(send_edges)
    edges = pieces[:, :edge_rows].reshape(groups, -1, edge_block, state_dim).transpose(0, 2, 1, 3)
    edges = edges.reshape(groups * edge_block, -1)
    rows_in = tokens.astype(F32)
    normed = (rows_in * lax.rsqrt(jnp.mean(rows_in * rows_in, axis=-1, keepdims=True) + EPS) * pre_gain).astype(BF16)
    comes_from = jnp.argmax(mig_dest[None, :] == mig_ids[:, None], axis=1)
    pieces = pieces[comes_from, edge_rows:]
    arrived = exchange(pieces)
    for step in behind:
        waiting, _ = lax.optimization_barrier((sent[step], pieces if step == groups - 2 else arrived))
        early_pages[step] = permute(waiting, "req", step)
    arrived = arrived.reshape(states.shape[1:])
    all_rows = lax.all_gather(normed, "head", axis=0, tiled=True)
    all_rows, inner_weight, _ = lax.optimization_barrier((all_rows, inner_weight, pieces))
    leaving = lax.dynamic_index_in_dim(mig_ids, request_index, 0, keepdims=False)
    target = jnp.argmax(reorder == leaving) // slots
    inner_flat = inner_weight.reshape(width, 2 * inner)
    inner_rows = jnp.dot(all_rows, inner_flat, preferred_element_type=F32).astype(BF16)
    shared_rows = jnp.dot(all_rows, shared_weight, preferred_element_type=F32).astype(BF16)

    lanes = slots * window

    def in_lanes(vector):
        return jnp.pad(vector, (0, lanes - heads)).reshape(1, lanes)

    moved, entry, readout, within, decay, gate, new_inner, new_shared = token_part(
        skip_gain,
        recv_rows,
        inner_rows,
        shared_rows,
        edges,
        jnp.repeat(counts, window).reshape(lanes, 1),
        conv_inner,
        conv_inner_bias.reshape(1, -1),
        conv_shared,
        conv_shared_bias.reshape(1, -1),
        in_lanes(step_bias),
        in_lanes(decay_log),
        window,
        heads,
        head_dim,
        state_dim,
        capacity,
    )
    late = exchange(lax.dynamic_update_index_in_dim(send_late, arrived, target, 0))
    edge_inner_out = new_inner.transpose(1, 0, 2)
    edge_shared_out = new_shared.transpose(1, 0, 2)

    states_out, messages = state_part(
        new_slots,
        slot_of,
        early_pages,
        list(range(groups)) if sent else [],
        late,
        states,
        moved,
        entry,
        readout,
        within,
        decay,
        gate,
        gate_gain.reshape(1, -1),
        out_weight,
        window,
        groups,
        shares,
    )
    messages = [permute(messages[step], "head", step) for step in range(shares - 1, 0, -1)] + [messages[0]]
    hidden_out = finish(tokens, messages, inner * shares)
    return (hidden_out, states_out, edge_inner_out, edge_shared_out)


def solution(mesh):
    placed = (
        P(("req", "head"), None),
        P(),
        P(None, None, "head"),
        P(),
        P(None, "head"),
        P("head"),
        P(),
        P(),
        P("head"),
        P("head"),
        P("head"),
        P("head"),
        P("head", None),
        P("req", "head", None, None),
        P("req", None, "head"),
        P("req", None, None),
        P("req"),
        P(),
        P(),
        P(),
    )
    return jax.shard_map(
        local,
        mesh=mesh,
        in_specs=placed,
        out_specs=(
            P(("req", "head"), None),
            P("req", "head", None, None),
            P("req", None, "head"),
            P("req", None, None),
        ),
        check_vma=False,
    )
```
